32 devices in a mesh: member: 16 (over z, y, x), pair: 2 (over core).
Axes of the slice: x: 2, y: 2, z: 4, core: 2. Of those that a mesh axis runs over, the one named last changes fastest.
Arguments:
- samples: bfloat16 [512, 512], replicated, may hold values from -6 to 6
- w_first: bfloat16 [16, 512, 2048], P('member', None, 'pair'), may hold values from -6 to 6
- b_first: bfloat16 [16, 2048], P('member', 'pair'), may hold values from -6 to 6
- w_second: bfloat16 [16, 2048, 2048], P('member', None, 'pair'), may hold values from -6 to 6
- b_second: bfloat16 [16, 2048], P('member', 'pair'), may hold values from -6 to 6
- w_third: bfloat16 [16, 2048, 64], P('member', 'pair'), may hold values from -6 to 6
- observed: float32 [512, 64], replicated, may hold values from -24 to 24
- perturb: float32 [16, 512, 64], P('member'), may hold values from -6 to 6
- variance: float32 [512, 64], replicated, may hold values from 32 to 1024
Outputs:
- new_first: bfloat16 [16, 512, 2048], P('member', None, 'pair')
- new_bfirst: bfloat16 [16, 2048], P('member', 'pair')
- new_second: bfloat16 [16, 2048, 2048], P('member', None, 'pair')
- new_bsecond: bfloat16 [16, 2048], P('member', 'pair')
- new_third: bfloat16 [16, 2048, 64], P('member', 'pair')
The draws below stay inside these ranges and needn't reach their ends.
All inputs are finite; a program needn't handle non-finite values.
Results may differ from the reference program's by a relative error of at most 0.019.
Values may be sent and summed in bfloat16 or wider, within the bound.
No kernel may reach another device: no remote copies, remote signals or barrier semaphores. Data moves between devices by JAX's collectives and lax.ppermute only.
A program may use at most 128 MiB of HBM per device.

```python
import math
import jax
import jax.numpy as jnp
from jax import lax

IN = 512
H = 2048
OUT = 64
S = 512
MEMBERS = 16


def block_levels(rng, dims, shards, smallest, high):
    level = 1.0
    for axis_at, parts in shards:
        draws = jax.random.uniform(jax.random.fold_in(jax.random.fold_in(rng, 6), axis_at), (parts,), jnp.float32, smallest / len(shards), high / len(shards))
        level = level * jnp.repeat(jnp.exp(draws), dims[axis_at] // parts).reshape((-1,) + (1,) * (len(dims) - 1 - axis_at))
    return level


def gaussian(rng, extent, scale, bound, split=(), kind=jnp.bfloat16):
    entries = jax.random.normal(rng, extent, jnp.float32) * scale
    if len(split) > 0:
        entries = block_levels(rng, extent, split, -0.22, 0.18) * entries
    return jnp.clip(entries, min=-bound, max=bound).astype(kind)


def setup_inputs(seed: int = 0) -> dict:
    arg_keys = jax.random.split(jax.random.key(seed), 10)
    samples = gaussian(arg_keys[0], (S, IN), 1.0, 6.0)
    w_first = gaussian(arg_keys[1], (MEMBERS, IN, H), 1.0, 6.0, ((0, 16), (2, 2)))
    b_first = gaussian(arg_keys[2], (MEMBERS, H), 1.0, 6.0, ((0, 16), (1, 2)))
    w_second = gaussian(arg_keys[3], (MEMBERS, H, H), 1.0, 6.0, ((0, 16), (2, 2)))
    b_second = gaussian(arg_keys[4], (MEMBERS, H), 1.0, 6.0, ((0, 16), (1, 2)))
    w_third = gaussian(arg_keys[5], (MEMBERS, H, OUT), 1.0, 6.0, ((0, 16), (1, 2)))
    observed = gaussian(arg_keys[6], (S, OUT), 4.0, 24.0, (), jnp.float32)
    perturb = gaussian(arg_keys[7], (MEMBERS, S, OUT), 1.0, 6.0, ((0, 16),), jnp.float32)
    variance = jnp.clip(jnp.exp(jax.random.uniform(arg_keys[8], (S, OUT), jnp.float32, math.log(32.0), math.log(1024.0))), 32.0, 1024.0)
    return dict(samples=samples, w_first=w_first, b_first=b_first, w_second=w_second, b_second=b_second, w_third=w_third, observed=observed, perturb=perturb, variance=variance)


def forward(samples, w_first, b_first, w_second, b_second, w_third):
    first = jax.nn.gelu(jnp.dot(samples.astype(jnp.float32), w_first.astype(jnp.float32), preferred_element_type=jnp.float32) * IN ** (-0.5) + b_first.astype(jnp.float32), approximate=True).astype(jnp.bfloat16)
    second = jax.nn.gelu(jnp.dot(first.astype(jnp.float32), w_second.astype(jnp.float32), preferred_element_type=jnp.float32) * H ** (-0.5) + b_second.astype(jnp.float32), approximate=True).astype(jnp.bfloat16)
    return jnp.dot(second.astype(jnp.float32), w_third.astype(jnp.float32), preferred_element_type=jnp.float32) * H ** (-0.5)

def solve_gain(amat, bmat):
    count = amat.shape[0]
    system = amat + count * jnp.eye(count, dtype=jnp.float32)
    factor = jnp.linalg.cholesky(system)
    middle = lax.linalg.triangular_solve(factor, bmat, left_side=True, lower=True, transpose_a=False)
    return lax.linalg.triangular_solve(factor, middle, left_side=True, lower=True, transpose_a=True)

def blend(theta, gain_low):
    count = theta.shape[0]
    per = theta.size // count
    width = math.gcd(per, 4096)
    blocks = theta.reshape(count, per // width, width).transpose(1, 0, 2)
    gain_tr = gain_low.T

    def mixone(block):
        full = block.astype(jnp.float32)
        center = (full - lax.optimization_barrier(jnp.mean(full, axis=0, keepdims=True))).astype(jnp.bfloat16)
        return jnp.dot(gain_tr.astype(jnp.float32), center.astype(jnp.float32), preferred_element_type=jnp.float32).astype(jnp.bfloat16)
    mixed = lax.map(mixone, blocks)
    return mixed.transpose(1, 0, 2).reshape(theta.shape)

def reference(samples, w_first, b_first, w_second, b_second, w_third, observed, perturb, variance):
    pred = lax.map(lambda p: forward(samples, p[0], p[1], p[2], p[3], p[4]), (w_first, b_first, w_second, b_second, w_third))
    resid = observed[None] + jnp.sqrt(variance)[None] * perturb - pred
    count = pred.shape[0]
    flatpred = pred.reshape(count, -1)
    flatres = resid.reshape(count, -1)
    devpred = flatpred - lax.optimization_barrier(jnp.mean(flatpred, axis=0, keepdims=True))
    scaled = devpred / variance.reshape(1, -1)
    amat = jnp.dot(scaled, devpred.T, precision=lax.Precision.HIGHEST)
    bmat = jnp.dot(scaled, flatres.T, precision=lax.Precision.HIGHEST)
    gain = solve_gain(amat, bmat)
    gain_low = gain.astype(jnp.bfloat16)
    return (blend(w_first, gain_low), blend(b_first, gain_low), blend(w_second, gain_low), blend(b_second, gain_low), blend(w_third, gain_low))
```

```python
import functools

import jax
import jax.numpy as jnp
from jax import lax
from jax.experimental import pallas as pl
from jax.experimental.pallas import tpu as pltpu
from jax.sharding import PartitionSpec as P

ROWS = 16
EARLY = 32
PLANE = 4
TILE = 256
LIGHT = pl.CostEstimate(flops=1, bytes_accessed=1, transcendentals=0)


def solve_gain(amat, bmat):
    count = amat.shape[0]
    system = amat + count * jnp.eye(count, dtype=jnp.float32)
    factor = jnp.linalg.cholesky(system)
    middle = lax.linalg.triangular_solve(
        factor, bmat, left_side=True, lower=True, transpose_a=False
    )
    return lax.linalg.triangular_solve(factor, middle, left_side=True, lower=True, transpose_a=True)


def mix_block(spread, x):
    members, rows, width = x.shape
    full = x.astype(jnp.float32)
    mean = jnp.sum(full, axis=0, keepdims=True) * (1.0 / members)
    center = (full - mean).astype(jnp.bfloat16).reshape(members * rows, width)
    mixed = jnp.dot(spread, center, preferred_element_type=jnp.float32)
    return mixed.astype(jnp.bfloat16).reshape(members, rows, width)


def mix_kernel(spread_ref, x_ref, y_ref):
    y_ref[...] = mix_block(spread_ref[...], x_ref[...])


def mix_two_kernel(split, spread_c_ref, spread_b_ref, c_ref, b_ref, y_ref):
    @pl.when(pl.program_id(0) < split)
    def _():
        y_ref[...] = mix_block(spread_c_ref[...], c_ref[...])

    @pl.when(pl.program_id(0) >= split)
    def _():
        y_ref[...] = mix_block(spread_b_ref[...], b_ref[...])


def spread_gain(gain_tr):
    members = gain_tr.shape[0]
    size = members * ROWS
    row = lax.broadcasted_iota(jnp.int32, (size, members), 0)
    col = lax.broadcasted_iota(jnp.int32, (size, members), 1)
    expand = (row // ROWS == col).astype(jnp.bfloat16)
    wide = jnp.dot(expand, gain_tr, preferred_element_type=jnp.float32).astype(jnp.bfloat16)
    wide = lax.dot_general(
        wide, expand, (((1,), (1,)), ((), ())), preferred_element_type=jnp.float32
    ).astype(jnp.bfloat16)
    at_row = lax.broadcasted_iota(jnp.int32, (size, size), 0) % ROWS
    at_col = lax.broadcasted_iota(jnp.int32, (size, size), 1) % ROWS
    return jnp.where(at_row == at_col, wide, jnp.bfloat16(0))


def mix_plain(slab, gain_tr):
    full = slab.astype(jnp.float32)
    center = (full - jnp.mean(full, axis=0, keepdims=True)).astype(jnp.bfloat16)
    return jnp.einsum(
        "jk,krc->jrc", gain_tr, center, preferred_element_type=jnp.float32
    ).astype(jnp.bfloat16)


def mix(slab, spread):
    members, rows, width = slab.shape
    block = pl.BlockSpec((members, ROWS, width), lambda i: (0, i, 0))
    return pl.pallas_call(
        mix_kernel,
        grid=(rows // ROWS,),
        in_specs=[pl.BlockSpec(spread.shape, lambda i: (0, 0)), block],
        out_specs=block,
        out_shape=jax.ShapeDtypeStruct(slab.shape, jnp.bfloat16),
        compiler_params=pltpu.CompilerParams(vmem_limit_bytes=32 << 20),
        cost_estimate=LIGHT,
    )(spread, slab)


def mix_two(slab_c, spread_c, slab_b, kept, spread_b):
    members, rows, width = slab_c.shape
    split = rows // ROWS
    rows = rows + kept
    out = jax.ShapeDtypeStruct((members, rows, width), jnp.bfloat16)
    whole = pl.BlockSpec(spread_c.shape, lambda i: (0, 0))
    shape = (members, ROWS, width)
    return pl.pallas_call(
        functools.partial(mix_two_kernel, split),
        grid=(rows // ROWS,),
        in_specs=[
            whole,
            whole,
            pl.BlockSpec(shape, lambda i: (0, jnp.minimum(i, split - 1), 0)),
            pl.BlockSpec(shape, lambda i: (0, jnp.maximum(i - split, 0), 0)),
        ],
        out_specs=pl.BlockSpec(shape, lambda i: (0, i, 0)),
        out_shape=out,
        compiler_params=pltpu.CompilerParams(vmem_limit_bytes=32 << 20),
        cost_estimate=LIGHT,
    )(spread_c, spread_b, slab_c, slab_b)


def first_kernel(scale, x_ref, w_ref, b_ref, y_ref):
    summed = jnp.dot(x_ref[...], w_ref[...], preferred_element_type=jnp.float32)
    y = jax.nn.gelu(summed * scale + b_ref[...].astype(jnp.float32), approximate=True)
    y_ref[...] = y.astype(jnp.bfloat16)


def first_layer(x, w, b):
    rows, depth = x.shape
    step = min(TILE, w.shape[1])
    return pl.pallas_call(
        functools.partial(first_kernel, depth ** (-0.5)),
        grid=(w.shape[1] // step,),
        in_specs=[
            pl.BlockSpec((rows, depth), lambda i: (0, 0)),
            pl.BlockSpec((depth, step), lambda i: (0, i)),
            pl.BlockSpec((1, step), lambda i: (0, i)),
        ],
        out_specs=pl.BlockSpec((rows, step), lambda i: (0, i)),
        out_shape=jax.ShapeDtypeStruct((rows, w.shape[1]), jnp.bfloat16),
        compiler_params=pltpu.CompilerParams(vmem_limit_bytes=32 << 20),
        cost_estimate=LIGHT,
    )(x, w, b)


def second_kernel(scale, side_ref, mine_ref, other_ref, wm_ref, wo_ref, b_ref, third_ref, y_ref):
    summed = jnp.dot(mine_ref[...], wm_ref[...], preferred_element_type=jnp.float32)
    summed += jnp.dot(other_ref[...], wo_ref[...], preferred_element_type=jnp.float32)
    y = jax.nn.gelu(summed * scale + b_ref[...].astype(jnp.float32), approximate=True)
    part = lax.dot_general(
        third_ref[...],
        y.astype(jnp.bfloat16),
        (((1,), (1,)), ((), ())),
        preferred_element_type=jnp.float32,
    )

    @pl.when(pl.program_id(0) == 0)
    def _():
        y_ref[...] = jnp.zeros_like(y_ref)

    y_ref[...] += part * scale


def second_and_third(side, mine, other, w, b, third):
    rows, depth = mine.shape
    outs = third.shape[0]
    step = min(TILE, w.shape[1])
    return pl.pallas_call(
        functools.partial(second_kernel, w.shape[0] ** (-0.5)),
        grid_spec=pltpu.PrefetchScalarGridSpec(
            num_scalar_prefetch=1,
            grid=(w.shape[1] // step,),
            in_specs=[
                pl.BlockSpec((rows, depth), lambda i, side: (0, 0)),
                pl.BlockSpec((rows, depth), lambda i, side: (0, 0)),
                pl.BlockSpec((depth, step), lambda i, side: (side[0], i)),
                pl.BlockSpec((depth, step), lambda i, side: (1 - side[0], i)),
                pl.BlockSpec((1, step), lambda i, side: (0, i)),
                pl.BlockSpec((outs, step), lambda i, side: (0, i)),
            ],
            out_specs=pl.BlockSpec((outs, rows), lambda i, side: (0, 0)),
        ),
        out_shape=jax.ShapeDtypeStruct((outs, rows), jnp.float32),
        compiler_params=pltpu.CompilerParams(vmem_limit_bytes=32 << 20),
        cost_estimate=LIGHT,
    )(side[None], mine, other, w, w, b, third)


def exchange(x):
    return lax.all_to_all(x, "member", split_axis=0, concat_axis=0, tiled=True)


def swap(x, axis, bit):
    count = lax.axis_size(axis)
    return lax.ppermute(x, axis, [(i, i ^ bit) for i in range(count)])


def reorder(gain_tr, order):
    pick = (order[None, :] == jnp.arange(gain_tr.shape[1])[:, None]).astype(jnp.bfloat16)
    return jnp.dot(gain_tr, pick, preferred_element_type=jnp.float32).astype(jnp.bfloat16)


def pick(x, at, axis=0):
    return lax.dynamic_index_in_dim(x, at, axis, keepdims=False)


def after(value, earlier):
    return lax.optimization_barrier((value, earlier))[0]


def body(samples, w_first, b_first, w_second, b_second, w_third, observed, perturb, variance):
    members = lax.axis_size("member")
    me = lax.axis_index("member")
    side = lax.axis_index("pair")
    width = w_first.shape[2]
    first_w, second_w, third_w = w_first[0], w_second[0], w_third[0]
    slabs_first = first_w.reshape(members, -1, width)
    slabs_second = second_w.reshape(members, -1, width)
    outs = third_w.shape[1]
    fast = members == PLANE * PLANE and outs % members == 0 and EARLY < slabs_second.shape[1]
    planes = members // PLANE
    plane, place = me // PLANE, me % PLANE

    def across(slabs, flip):
        blocks = slabs.reshape((planes, PLANE) + slabs.shape[1:])
        return swap(pick(blocks, plane ^ flip), "member", flip * PLANE)

    def within(parts):
        got = []
        for flip in range(PLANE):
            block = jnp.stack([pick(part, place ^ flip) for part in parts])
            got.append(swap(block, "member", flip) if flip else block)
        return got

    def own_plane(slabs):
        return pick(slabs.reshape((planes, PLANE) + slabs.shape[1:]), plane)

    first = first_layer(samples, first_w, b_first)
    partial_out = second_and_third(
        side, first, swap(first, "pair", 1), second_w, b_second, third_w.T
    )

    half = partial_out.shape[1] // 2
    start = side * half
    keep = lax.dynamic_slice_in_dim(partial_out, start, half, 1)
    give = lax.dynamic_slice_in_dim(partial_out, (1 - side) * half, half, 1)
    pred = keep + swap(give, "pair", 1)
    observed_half = lax.dynamic_slice_in_dim(observed.T, start, half, 1)
    variance_half = lax.dynamic_slice_in_dim(variance.T, start, half, 1)
    perturb_half = lax.dynamic_slice_in_dim(perturb[0].T, start, half, 1)
    resid = observed_half + jnp.sqrt(variance_half) * perturb_half - pred
    count = pred.size // members
    both = jnp.concatenate(
        [pred.reshape(members, 1, count), resid.reshape(members, 1, count)], axis=1
    )
    if fast:
        early = slabs_second[:, :EARLY]
        biases = jnp.concatenate([b_first.reshape(members, -1), b_second.reshape(members, -1)], 1)
        biases = jnp.pad(biases, ((0, 0), (0, width - biases.shape[1])))
        small = jnp.concatenate([third_w.T.reshape(members, -1, width), biases[:, None]], axis=1)
        small = jnp.pad(small, ((0, 0), (0, -small.shape[1] % 8), (0, 0)))
        late = jnp.concatenate([slabs_second[:, EARLY:], small], axis=1)
        parts = [own_plane(slabs_first)] + [across(slabs_first, i) for i in range(1, planes)]
        both, parts, late, early = lax.optimization_barrier((both, parts, late, early))
        both, got_first, far2 = lax.optimization_barrier(
            (exchange(both), within(parts), across(early, 2))
        )
    else:
        both = exchange(both)
    allpred, allres = both[:, 0], both[:, 1]
    var_part = lax.dynamic_index_in_dim(variance_half.reshape(members, count), me, 0)
    devpred = allpred - jnp.mean(allpred, axis=0, keepdims=True)
    scaled = devpred / var_part
    sums = jnp.dot(
        scaled, jnp.concatenate([devpred, allres], axis=0).T, precision=lax.Precision.HIGHEST
    )
    if fast:
        sums = sums + swap(sums, "pair", 1)
        sums = jnp.broadcast_to(sums[None], (members,) + sums.shape)
        sums, early = lax.optimization_barrier((sums, early))
        sums, far1, far3 = lax.optimization_barrier(
            (exchange(sums), across(early, 1), across(early, 3))
        )
        sums = jnp.sum(sums, axis=0)
        got_late = exchange(after(late, sums))
    else:
        sums = lax.psum(sums, ("member", "pair"))

    gain = solve_gain(sums[:, :members], sums[:, members:])
    gain_tr = gain.astype(jnp.bfloat16).T
    if fast:
        flips = jnp.arange(members)
        order = me ^ (flips // planes + flips % planes * PLANE)
        gain_in = reorder(gain_tr, order)
        spread = spread_gain(gain_tr)
        spread_in = spread_gain(gain_in)
        spread_both = spread_gain(reorder(gain_in.T, order).T)

        mixed_first = mix(jnp.concatenate(got_first, axis=0), spread_both)
        mixed_first = mixed_first.reshape((PLANE, planes) + mixed_first.shape[1:])
        back = jnp.stack(
            [mixed_first[0]] + [swap(mixed_first[i], "member", i) for i in range(1, PLANE)]
        )
        early_parts = after([own_plane(early), far1, far2, far3], mixed_first)
        got_early = within(early_parts)
        back, got_late, got_early = lax.optimization_barrier((back, got_late, got_early))
        homes = []
        for flip in range(planes):
            block = jnp.stack([pick(back, place ^ i)[flip] for i in range(PLANE)])
            homes.append(swap(block, "member", flip * PLANE) if flip else block)

        kept = slabs_second.shape[1] - EARLY
        mixed_second = mix_two(
            jnp.concatenate(got_early, axis=0), spread_in, got_late, kept, spread
        )
        mixed_small = mix_plain(got_late[:, kept:], gain_tr)
        mixed_second = jnp.concatenate([mixed_second, mixed_small], axis=1)
        mixed_second, homes = lax.optimization_barrier((mixed_second, homes))
        new_second = exchange(mixed_second)
        new_first = jnp.zeros(first_w.shape, jnp.bfloat16)
        size = first_w.shape[0] // planes
        for flip, home in enumerate(homes):
            new_first = lax.dynamic_update_slice_in_dim(
                new_first, home.reshape(size, width), (plane ^ flip) * size, 0
            )
        new_small = new_second[:, kept + EARLY :]
        new_second = new_second[:, : kept + EARLY]
        rows = outs // members
        new_third = new_small[:, :rows].reshape(outs, width).T
        cut = width // members
        new_bfirst = new_small[:, rows, :cut].reshape(b_first.shape)
        new_bsecond = new_small[:, rows, cut : 2 * cut].reshape(b_second.shape)
    else:
        new_first = exchange(mix_plain(exchange(slabs_first), gain_tr))
        new_second = exchange(mix_plain(exchange(slabs_second), gain_tr))
        small = jnp.concatenate([third_w.T, b_first, b_second], axis=0)
        full = lax.all_gather(small, "member", axis=0)
        new_small = mix_plain(full, lax.dynamic_index_in_dim(gain_tr, me, 0))[0]
        new_third = new_small[:outs].T
        new_bfirst = new_small[outs : outs + 1]
        new_bsecond = new_small[outs + 1 :]
    return (
        new_first.reshape(w_first.shape),
        new_bfirst,
        new_second.reshape(w_second.shape),
        new_bsecond,
        new_third[None],
    )


def solution(mesh):
    in_specs = (
        P(),
        P("member", None, "pair"),
        P("member", "pair"),
        P("member", None, "pair"),
        P("member", "pair"),
        P("member", "pair", None),
        P(),
        P("member", None, None),
        P(),
    )
    out_specs = (
        P("member", None, "pair"),
        P("member", "pair"),
        P("member", None, "pair"),
        P("member", "pair"),
        P("member", "pair", None),
    )
    return jax.shard_map(body, mesh=mesh, in_specs=in_specs, out_specs=out_specs, check_vma=False)
```

```python
import functools

import jax
import jax.numpy as jnp
from jax import lax
from jax.experimental import pallas as pl
from jax.experimental.pallas import tpu as pltpu
from jax.sharding import PartitionSpec as P

ROWS = 16
PLANE = 4
TILE = 256
VMEM = 56 << 20
LIGHT = pl.CostEstimate(flops=1, bytes_accessed=1, transcendentals=0)


def solve_gain(amat, bmat):
    count = amat.shape[0]
    system = amat + count * jnp.eye(count, dtype=jnp.float32)
    factor = jnp.linalg.cholesky(system)
    middle = lax.linalg.triangular_solve(
        factor, bmat, left_side=True, lower=True, transpose_a=False
    )
    return lax.linalg.triangular_solve(factor, middle, left_side=True, lower=True, transpose_a=True)


def mix_kernel(spread_ref, x_ref, y_ref):
    members, rows, width = x_ref.shape
    for at in range(0, rows, ROWS):
        for left in range(0, width, TILE):
            piece = (slice(None), pl.ds(at, ROWS), pl.ds(left, TILE))
            full = x_ref[piece].astype(jnp.float32)
            mean = jnp.sum(full, axis=0, keepdims=True) * (1.0 / members)
            center = (full - mean).astype(jnp.bfloat16).reshape(members * ROWS, TILE)
            mixed = jnp.dot(spread_ref[...], center, preferred_element_type=jnp.float32)
            y_ref[piece] = mixed.astype(jnp.bfloat16).reshape(members, ROWS, TILE)


def copy_kernel(x_ref, y_ref):
    y_ref[...] = x_ref[...]


def blocked(kernel, x, *wholes):
    members, total, width = x.shape
    rows = min(total, 4 * ROWS)
    block = pl.BlockSpec((members, rows, width), lambda i: (0, i, 0))
    return pl.pallas_call(
        kernel,
        grid=(total // rows,),
        in_specs=[pl.BlockSpec(w.shape, lambda i: (0, 0)) for w in wholes] + [block],
        out_specs=block,
        out_shape=jax.ShapeDtypeStruct(x.shape, jnp.bfloat16),
        compiler_params=pltpu.CompilerParams(vmem_limit_bytes=VMEM),
        cost_estimate=LIGHT,
    )(*wholes, x)


def moments_kernel(both_ref, var_ref, sums_ref):
    pred, resid = both_ref[:, 0, :], both_ref[:, 1, :]
    dev = pred - jnp.sum(pred, axis=0, keepdims=True) * (1.0 / pred.shape[0])
    scaled = dev / var_ref[...]
    sums_ref[...] = lax.dot_general(
        scaled,
        jnp.concatenate([dev, resid], axis=0),
        (((1,), (1,)), ((), ())),
        precision=lax.Precision.HIGHEST,
        preferred_element_type=jnp.float32,
    )


def whole_call(kernel, out_shape, *args):
    return pl.pallas_call(kernel, out_shape=out_shape, cost_estimate=LIGHT)(*args)


def solve_kernel(sums_ref, gain_ref, spread_ref):
    total = sums_ref[...]
    count = total.shape[0]
    row = lax.broadcasted_iota(jnp.int32, total.shape, 0)
    col = lax.broadcasted_iota(jnp.int32, total.shape, 1)
    total = total + jnp.where(row == col, float(count), 0.0)
    for k in range(count):
        pivot = total[k : k + 1, :] / total[k : k + 1, k : k + 1]
        factor = jnp.where(row == k, total - 1.0, total)[:, k : k + 1]
        total = total - factor * pivot
    gain = total[:, count:].astype(jnp.bfloat16)
    gain_ref[...] = gain
    size = count * ROWS
    row = lax.broadcasted_iota(jnp.int32, (size, count), 0)
    col = lax.broadcasted_iota(jnp.int32, (size, count), 1)
    expand = (row // ROWS == col).astype(jnp.bfloat16)
    wide = lax.dot_general(
        expand, gain, (((1,), (1,)), ((), ())), preferred_element_type=jnp.float32
    ).astype(jnp.bfloat16)
    wide = lax.dot_general(
        wide, expand, (((1,), (1,)), ((), ())), preferred_element_type=jnp.float32
    )
    at_row = lax.broadcasted_iota(jnp.int32, (size, size), 0) % ROWS
    at_col = lax.broadcasted_iota(jnp.int32, (size, size), 1) % ROWS
    spread_ref[...] = jnp.where(at_row == at_col, wide, 0.0).astype(jnp.bfloat16)


def spread_gain(gain_tr):
    members = gain_tr.shape[0]
    size = members * ROWS
    row = lax.broadcasted_iota(jnp.int32, (size, members), 0)
    col = lax.broadcasted_iota(jnp.int32, (size, members), 1)
    expand = (row // ROWS == col).astype(jnp.bfloat16)
    wide = jnp.dot(expand, gain_tr, preferred_element_type=jnp.float32).astype(jnp.bfloat16)
    wide = lax.dot_general(
        wide, expand, (((1,), (1,)), ((), ())), preferred_element_type=jnp.float32
    ).astype(jnp.bfloat16)
    at_row = lax.broadcasted_iota(jnp.int32, (size, size), 0) % ROWS
    at_col = lax.broadcasted_iota(jnp.int32, (size, size), 1) % ROWS
    return jnp.where(at_row == at_col, wide, jnp.bfloat16(0))


def mix_plain(slab, gain_tr):
    full = slab.astype(jnp.float32)
    center = (full - jnp.mean(full, axis=0, keepdims=True)).astype(jnp.bfloat16)
    return jnp.einsum(
        "jk,krc->jrc", gain_tr, center, preferred_element_type=jnp.float32
    ).astype(jnp.bfloat16)


def mix_one_kernel(column_ref, *refs):
    y_ref = refs[-1]
    blocks = [ref[...].astype(jnp.float32) for ref in refs[:-1]]
    members = column_ref.shape[0]
    mean = sum(jnp.sum(block, axis=0) for block in blocks) * (1.0 / members)
    total = jnp.zeros_like(mean)
    at = 0
    for block in blocks:
        for i in range(block.shape[0]):
            center = (block[i] - mean).astype(jnp.bfloat16).astype(jnp.float32)
            total = total + center * column_ref[at]
            at += 1
    y_ref[...] = total.astype(jnp.bfloat16)


def mix_one(column, blocks):
    rows, width = blocks[0].shape[1:]
    step = rows if rows % ROWS else ROWS
    return pl.pallas_call(
        mix_one_kernel,
        grid=(rows // step,),
        in_specs=[pl.BlockSpec(memory_space=pltpu.SMEM)]
        + [pl.BlockSpec((x.shape[0], step, width), lambda i: (0, i, 0)) for x in blocks],
        out_specs=pl.BlockSpec((step, width), lambda i: (i, 0)),
        out_shape=jax.ShapeDtypeStruct((rows, width), jnp.bfloat16),
        compiler_params=pltpu.CompilerParams(vmem_limit_bytes=VMEM),
        cost_estimate=LIGHT,
    )(column, *blocks)


def first_kernel(scale, x_ref, w_ref, b_ref, y_ref):
    summed = jnp.dot(x_ref[...], w_ref[...], preferred_element_type=jnp.float32)
    y = jax.nn.gelu(summed * scale + b_ref[...].astype(jnp.float32), approximate=True)
    y_ref[...] = y.astype(jnp.bfloat16)


def first_layer(x, w, b, part):
    rows, depth = x.shape
    half = w.shape[1] // 2
    step = min(TILE, half)
    first = part * (half // step)
    return pl.pallas_call(
        functools.partial(first_kernel, depth ** (-0.5)),
        grid=(half // step,),
        in_specs=[
            pl.BlockSpec((rows, depth), lambda i: (0, 0)),
            pl.BlockSpec((depth, step), lambda i: (0, i + first)),
            pl.BlockSpec((1, step), lambda i: (0, i + first)),
        ],
        out_specs=pl.BlockSpec((rows, step), lambda i: (0, i)),
        out_shape=jax.ShapeDtypeStruct((rows, half), jnp.bfloat16),
        compiler_params=pltpu.CompilerParams(vmem_limit_bytes=32 << 20),
        cost_estimate=LIGHT,
    )(x, w, b)


def second_kernel(scale, side_ref, *refs):
    inputs, weights, (b_ref, third_ref, y_ref) = refs[:4], refs[4:8], refs[8:]
    summed = sum(
        jnp.dot(x_ref[...], w_ref[...], preferred_element_type=jnp.float32)
        for x_ref, w_ref in zip(inputs, weights)
    )
    y = jax.nn.gelu(summed * scale + b_ref[...].astype(jnp.float32), approximate=True)
    part = lax.dot_general(
        third_ref[...],
        y.astype(jnp.bfloat16),
        (((1,), (1,)), ((), ())),
        preferred_element_type=jnp.float32,
    )

    @pl.when(pl.program_id(0) == 0)
    def _():
        y_ref[...] = jnp.zeros_like(y_ref)

    y_ref[...] += part * scale


def second_and_third(side, mine, other, w, b, third):
    rows, depth = mine[0].shape
    outs = third.shape[0]
    step = min(TILE, w.shape[1])
    whole = pl.BlockSpec((rows, depth), lambda i, side: (0, 0))
    return pl.pallas_call(
        functools.partial(second_kernel, w.shape[0] ** (-0.5)),
        grid_spec=pltpu.PrefetchScalarGridSpec(
            num_scalar_prefetch=1,
            grid=(w.shape[1] // step,),
            in_specs=[whole] * 4
            + [
                pl.BlockSpec((depth, step), lambda i, side: (2 * side[0], i)),
                pl.BlockSpec((depth, step), lambda i, side: (2 * side[0] + 1, i)),
                pl.BlockSpec((depth, step), lambda i, side: (2 - 2 * side[0], i)),
                pl.BlockSpec((depth, step), lambda i, side: (3 - 2 * side[0], i)),
                pl.BlockSpec((1, step), lambda i, side: (0, i)),
                pl.BlockSpec((outs, step), lambda i, side: (0, i)),
            ],
            out_specs=pl.BlockSpec((outs, rows), lambda i, side: (0, 0)),
        ),
        out_shape=jax.ShapeDtypeStruct((outs, rows), jnp.float32),
        compiler_params=pltpu.CompilerParams(vmem_limit_bytes=32 << 20),
        cost_estimate=LIGHT,
    )(side[None], *mine, *other, w, w, w, w, b, third)


def exchange(x):
    return lax.all_to_all(x, "member", split_axis=0, concat_axis=0, tiled=True)


def swap(x, axis, bit):
    count = lax.axis_size(axis)
    return lax.ppermute(x, axis, [(i, i ^ bit) for i in range(count)])


def reorder(gain_tr, order):
    pick = (order[None, :] == jnp.arange(gain_tr.shape[1])[:, None]).astype(jnp.bfloat16)
    return jnp.dot(gain_tr, pick, preferred_element_type=jnp.float32).astype(jnp.bfloat16)


def pick(x, at, axis=0):
    return lax.dynamic_index_in_dim(x, at, axis, keepdims=False)


def after(value, earlier):
    return lax.optimization_barrier((value, earlier))[0]


def body(samples, w_first, b_first, w_second, b_second, w_third, observed, perturb, variance):
    members = lax.axis_size("member")
    me = lax.axis_index("member")
    side = lax.axis_index("pair")
    width = w_first.shape[2]
    first_w, second_w, third_w = w_first[0], w_second[0], w_third[0]
    slabs_first = first_w.reshape(members, -1, width)
    slabs_second = second_w.reshape(members, -1, width)
    outs = third_w.shape[1]
    fast = members == PLANE * PLANE and width % TILE == 0
    planes = members // PLANE
    plane, place = me // PLANE, me % PLANE

    def across(x, flip):
        return swap(x, "member", flip * PLANE)

    first = [first_layer(samples, first_w, b_first, i) for i in range(2)]
    other = [swap(x, "pair", 1) for x in first]
    partial_out = second_and_third(side, first, other, second_w, b_second, third_w.T)

    half = partial_out.shape[1] // 2
    start = side * half
    keep = lax.dynamic_slice_in_dim(partial_out, start, half, 1)
    give = lax.dynamic_slice_in_dim(partial_out, (1 - side) * half, half, 1)
    pred = keep + swap(give, "pair", 1)
    observed_half = lax.dynamic_slice_in_dim(observed.T, start, half, 1)
    variance_half = lax.dynamic_slice_in_dim(variance.T, start, half, 1)
    perturb_half = lax.dynamic_slice_in_dim(perturb[0].T, start, half, 1)
    resid = observed_half + jnp.sqrt(variance_half) * perturb_half - pred
    count = pred.size // members
    both = jnp.concatenate(
        [pred.reshape(members, 1, count), resid.reshape(members, 1, count)], axis=1
    )
    got_first = exchange(slabs_first)
    var_part = lax.dynamic_index_in_dim(variance_half.reshape(members, count), me, 0)
    if fast:
        both = both.reshape((planes, PLANE) + both.shape[1:])
        parts = [pick(both, plane ^ i) for i in range(planes)]
        parts = jnp.stack([parts[0]] + [across(parts[i], i) for i in range(1, planes)])
        pad = jnp.zeros((-(outs + 2) % 8, width), jnp.bfloat16)
        small = jnp.concatenate([third_w.T, b_first, b_second, pad], axis=0)[None]
        held = [small, swap(after(small, both), "member", 8)]
        slabs_second, parts, held[1], got_first = lax.optimization_barrier(
            (slabs_second, parts, held[1], got_first)
        )
        got_second = exchange(slabs_second)
        held.append(swap(jnp.concatenate(held, axis=0), "member", 4))
        both = jnp.stack([pick(parts, plane ^ i) for i in range(planes)])
        parts = [pick(both, place ^ i, 1) for i in range(PLANE)]
        parts = jnp.stack([parts[0]] + [swap(parts[i], "member", i) for i in range(1, PLANE)])
        both = jnp.stack([pick(parts, place ^ i) for i in range(PLANE)], axis=1)
        both = both.reshape((members,) + both.shape[2:])
        sums = whole_call(
            moments_kernel,
            jax.ShapeDtypeStruct((members, 2 * members), jnp.float32),
            both,
            var_part,
        )
        sums = sums + swap(sums, "pair", 1)
        sums = sums + swap(sums, "member", 1)
        sums = sums + swap(sums, "member", 2)
        held[2] = after(held[2], sums)
        held.append(swap(jnp.concatenate(held, axis=0), "member", 2))
        far = [across(sums, i) for i in range(1, planes)]
        sums, got_second = lax.optimization_barrier(
            ((sums + far[0]) + (far[1] + far[2]), got_second)
        )
        gain, spread = whole_call(
            solve_kernel,
            [
                jax.ShapeDtypeStruct((members, members), jnp.bfloat16),
                jax.ShapeDtypeStruct((members * ROWS, members * ROWS), jnp.bfloat16),
            ],
            sums,
        )
        mixed_second = blocked(mix_kernel, got_second, spread)
        mixed_second, got_first, held[3] = lax.optimization_barrier(
            (mixed_second, got_first, held[3])
        )
        new_second = exchange(mixed_second)

        mixed_first = blocked(mix_kernel, got_first, spread)
        mixed_first = mixed_first.reshape((planes, PLANE) + mixed_first.shape[1:])
        parts = [pick(mixed_first, place ^ i, 1) for i in range(PLANE)]
        parts = jnp.stack([parts[0]] + [swap(parts[i], "member", i) for i in range(1, PLANE)])
        held[3] = after(held[3], parts)
        held.append(swap(jnp.concatenate(held, axis=0), "member", 1))
        homes = []
        for flip in range(planes):
            block = jnp.stack([pick(pick(parts, place ^ i), plane ^ flip) for i in range(PLANE)])
            homes.append(across(block, flip) if flip else block)

        order = me[None]
        for bit in (8, 4, 2, 1):
            order = jnp.concatenate([order, order ^ bit])
        column = reorder(pick(gain, me, 1)[None], order)[0].astype(jnp.float32)
        new_small = mix_one(column, held)
        new_third = new_small[:outs].T
        new_bfirst = new_small[outs : outs + 1]
        new_bsecond = new_small[outs + 1 : outs + 2]
        new_second = blocked(copy_kernel, new_second)
        homes, new_second, new_third, new_bfirst, new_bsecond = lax.optimization_barrier(
            (homes, new_second, new_third, new_bfirst, new_bsecond)
        )
        new_first = jnp.zeros(slabs_first.shape, jnp.bfloat16)
        for flip, part in enumerate(homes):
            new_first = lax.dynamic_update_slice_in_dim(
                new_first, part, (plane ^ flip) * PLANE, 0
            )
    else:
        both = exchange(both)
        allpred, allres = both[:, 0], both[:, 1]
        devpred = allpred - jnp.mean(allpred, axis=0, keepdims=True)
        scaled = devpred / var_part
        sums = jnp.dot(
            scaled, jnp.concatenate([devpred, allres], axis=0).T, precision=lax.Precision.HIGHEST
        )
        sums = lax.psum(sums, ("member", "pair"))
        gain = solve_gain(sums[:, :members], sums[:, members:])
        gain_tr = gain.astype(jnp.bfloat16).T
        new_second = exchange(mix_plain(exchange(slabs_second), gain_tr))
        new_first = exchange(mix_plain(got_first, gain_tr))
        small = jnp.concatenate([third_w.T, b_first, b_second], axis=0)
        full = lax.all_gather(small, "member", axis=0)
        new_small = mix_plain(full, lax.dynamic_index_in_dim(gain_tr, me, 0))[0]
        new_third = new_small[:outs].T
        new_bfirst = new_small[outs : outs + 1]
        new_bsecond = new_small[outs + 1 :]
    return (
        new_first.reshape(w_first.shape),
        new_bfirst,
        new_second.reshape(w_second.shape),
        new_bsecond,
        new_third[None],
    )


def solution(mesh):
    in_specs = (
        P(),
        P("member", None, "pair"),
        P("member", "pair"),
        P("member", None, "pair"),
        P("member", "pair"),
        P("member", "pair", None),
        P(),
        P("member", None, None),
        P(),
    )
    out_specs = (
        P("member", None, "pair"),
        P("member", "pair"),
        P("member", None, "pair"),
        P("member", "pair"),
        P("member", "pair", None),
    )
    return jax.shard_map(body, mesh=mesh, in_specs=in_specs, out_specs=out_specs, check_vma=False)
```

```python
import functools

import jax
import jax.numpy as jnp
from jax import lax
from jax.experimental import pallas as pl
from jax.experimental.pallas import tpu as pltpu
from jax.sharding import PartitionSpec as P

ROW_BITS = 4
ROWS = 1 << ROW_BITS
PLANE = 4
TILE = 256
VMEM = 56 << 20
LIGHT = pl.CostEstimate(flops=1, bytes_accessed=1, transcendentals=0)


def solve_gain(amat, bmat):
    count = amat.shape[0]
    system = amat + count * jnp.eye(count, dtype=jnp.float32)
    factor = jnp.linalg.cholesky(system)
    middle = lax.linalg.triangular_solve(
        factor, bmat, left_side=True, lower=True, transpose_a=False
    )
    return lax.linalg.triangular_solve(factor, middle, left_side=True, lower=True, transpose_a=True)


def mix_rows(spread_ref, x_ref, y_ref, at):
    members, _, width = x_ref.shape
    for left in range(0, width, TILE):
        piece = (slice(None), pl.ds(at, ROWS), pl.ds(left, TILE))
        full = x_ref[piece].astype(jnp.float32)
        mean = jnp.sum(full, axis=0, keepdims=True) * (1.0 / members)
        center = (full - mean).astype(jnp.bfloat16).reshape(members * ROWS, TILE)
        mixed = jnp.dot(spread_ref[...], center, preferred_element_type=jnp.float32)
        y_ref[piece] = mixed.astype(jnp.bfloat16).reshape(members, ROWS, TILE)


def mix_kernel(spread_ref, x_ref, y_ref):
    for at in range(0, x_ref.shape[1], ROWS):
        mix_rows(spread_ref, x_ref, y_ref, at)


def copy_kernel(x_ref, y_ref):
    y_ref[...] = x_ref[...]


def blocked(kernel, x, *wholes):
    members, total, width = x.shape
    rows = min(total, 4 * ROWS)
    block = pl.BlockSpec((members, rows, width), lambda i: (0, i, 0))
    return pl.pallas_call(
        kernel,
        grid=(total // rows,),
        in_specs=[pl.BlockSpec(w.shape, lambda i: (0, 0)) for w in wholes] + [block],
        out_specs=block,
        out_shape=jax.ShapeDtypeStruct(x.shape, jnp.bfloat16),
        compiler_params=pltpu.CompilerParams(vmem_limit_bytes=VMEM),
        cost_estimate=LIGHT,
    )(*wholes, x)


def moments_kernel(both_ref, var_ref, sums_ref):
    pred, resid = both_ref[:, 0, :], both_ref[:, 1, :]
    dev = pred - jnp.sum(pred, axis=0, keepdims=True) * (1.0 / pred.shape[0])
    scaled = dev / var_ref[...]
    sums_ref[...] = lax.dot_general(
        scaled,
        jnp.concatenate([dev, resid], axis=0),
        (((1,), (1,)), ((), ())),
        precision=lax.Precision.HIGHEST,
        preferred_element_type=jnp.float32,
    )


def whole_call(kernel, out_shape, *args):
    return pl.pallas_call(kernel, out_shape=out_shape, cost_estimate=LIGHT)(*args)


def solve_kernel(
    own_ref, far1_ref, far2_ref, far3_ref, x_ref, gain_ref, spread_ref, y_ref, x_buf, y_buf, x_sem, y_sems
):
    load = pltpu.make_async_copy(x_ref, x_buf, x_sem)
    load.start()
    total = (own_ref[...] + far1_ref[...]) + (far2_ref[...] + far3_ref[...])
    count = total.shape[0]
    row = lax.broadcasted_iota(jnp.int32, total.shape, 0)
    col = lax.broadcasted_iota(jnp.int32, total.shape, 1)
    total = total + jnp.where(row == col, float(count), 0.0)
    for k in range(count):
        pivot = total[k : k + 1, :] / total[k : k + 1, k : k + 1]
        factor = jnp.where(row == k, total - 1.0, total)[:, k : k + 1]
        total = total - factor * pivot
    gain = total[:, count:].astype(jnp.bfloat16)
    gain_ref[...] = gain
    size = count * ROWS
    row = lax.broadcasted_iota(jnp.int32, (size, count), 0)
    col = lax.broadcasted_iota(jnp.int32, (size, count), 1)
    expand = (row >> ROW_BITS == col).astype(jnp.bfloat16)
    wide = lax.dot_general(
        expand, gain, (((1,), (1,)), ((), ())), preferred_element_type=jnp.float32
    ).astype(jnp.bfloat16)
    wide = lax.dot_general(
        wide, expand, (((1,), (1,)), ((), ())), preferred_element_type=jnp.float32
    )
    at_row = lax.broadcasted_iota(jnp.int32, (size, size), 0)
    at_col = lax.broadcasted_iota(jnp.int32, (size, size), 1)
    same = ((at_row ^ at_col) & (ROWS - 1)) == 0
    spread_ref[...] = jnp.where(same, wide, 0.0).astype(jnp.bfloat16)

    load.wait()
    stores = []
    for i in range(x_ref.shape[1] // ROWS):
        rows = (slice(None), pl.ds(i * ROWS, ROWS), slice(None))
        mix_rows(spread_ref, x_buf, y_buf, i * ROWS)
        stores.append(pltpu.make_async_copy(y_buf.at[rows], y_ref.at[rows], y_sems.at[i]))
        stores[-1].start()
    for store in stores:
        store.wait()


def solve(sums, x):
    members = x.shape[0]
    size = members * ROWS
    vmem, anywhere = pl.BlockSpec(memory_space=pltpu.VMEM), pl.BlockSpec(memory_space=pl.ANY)
    return pl.pallas_call(
        solve_kernel,
        in_specs=[vmem] * len(sums) + [anywhere],
        out_specs=[vmem, vmem, anywhere],
        out_shape=[
            jax.ShapeDtypeStruct((members, members), jnp.bfloat16),
            jax.ShapeDtypeStruct((size, size), jnp.bfloat16),
            jax.ShapeDtypeStruct(x.shape, x.dtype),
        ],
        scratch_shapes=[
            pltpu.VMEM(x.shape, x.dtype),
            pltpu.VMEM(x.shape, x.dtype),
            pltpu.SemaphoreType.DMA,
            pltpu.SemaphoreType.DMA((x.shape[1] // ROWS,)),
        ],
        compiler_params=pltpu.CompilerParams(vmem_limit_bytes=VMEM),
        cost_estimate=LIGHT,
    )(*sums, x)


def mix_plain(slab, gain_tr):
    full = slab.astype(jnp.float32)
    center = (full - jnp.mean(full, axis=0, keepdims=True)).astype(jnp.bfloat16)
    return jnp.einsum(
        "jk,krc->jrc", gain_tr, center, preferred_element_type=jnp.float32
    ).astype(jnp.bfloat16)


def mix_one_kernel(column_ref, *refs):
    y_ref = refs[-1]
    blocks = [ref[...].astype(jnp.float32) for ref in refs[:-1]]
    members = column_ref.shape[0]
    mean = sum(jnp.sum(block, axis=0) for block in blocks) * (1.0 / members)
    total = jnp.zeros_like(mean)
    at = 0
    for block in blocks:
        for i in range(block.shape[0]):
            center = (block[i] - mean).astype(jnp.bfloat16).astype(jnp.float32)
            total = total + center * column_ref[at]
            at += 1
    y_ref[...] = total.astype(jnp.bfloat16)


def mix_one(column, blocks):
    rows, width = blocks[0].shape[1:]
    step = rows if rows % ROWS else ROWS
    return pl.pallas_call(
        mix_one_kernel,
        grid=(rows // step,),
        in_specs=[pl.BlockSpec(memory_space=pltpu.SMEM)]
        + [pl.BlockSpec((x.shape[0], step, width), lambda i: (0, i, 0)) for x in blocks],
        out_specs=pl.BlockSpec((step, width), lambda i: (i, 0)),
        out_shape=jax.ShapeDtypeStruct((rows, width), jnp.bfloat16),
        compiler_params=pltpu.CompilerParams(vmem_limit_bytes=VMEM),
        cost_estimate=LIGHT,
    )(column, *blocks)


def first_kernel(scale, x_ref, w_ref, b_ref, y_ref):
    summed = jnp.dot(x_ref[...], w_ref[...], preferred_element_type=jnp.float32)
    y = jax.nn.gelu(summed * scale + b_ref[...].astype(jnp.float32), approximate=True)
    y_ref[...] = y.astype(jnp.bfloat16)


def first_layer(x, w, b, part):
    rows, depth = x.shape
    half = w.shape[1] // 2
    step = min(TILE, half)
    first = part * (half // step)
    return pl.pallas_call(
        functools.partial(first_kernel, depth ** (-0.5)),
        grid=(half // step,),
        in_specs=[
            pl.BlockSpec((rows, depth), lambda i: (0, 0)),
            pl.BlockSpec((depth, step), lambda i: (0, i + first)),
            pl.BlockSpec((1, step), lambda i: (0, i + first)),
        ],
        out_specs=pl.BlockSpec((rows, step), lambda i: (0, i)),
        out_shape=jax.ShapeDtypeStruct((rows, half), jnp.bfloat16),
        compiler_params=pltpu.CompilerParams(vmem_limit_bytes=32 << 20),
        cost_estimate=LIGHT,
    )(x, w, b)


def second_kernel(scale, side_ref, *refs):
    inputs, weights, (b_ref, third_ref, y_ref) = refs[:4], refs[4:8], refs[8:]
    summed = sum(
        jnp.dot(x_ref[...], w_ref[...], preferred_element_type=jnp.float32)
        for x_ref, w_ref in zip(inputs, weights)
    )
    y = jax.nn.gelu(summed * scale + b_ref[...].astype(jnp.float32), approximate=True)
    part = lax.dot_general(
        third_ref[...],
        y.astype(jnp.bfloat16),
        (((1,), (1,)), ((), ())),
        preferred_element_type=jnp.float32,
    )

    @pl.when(pl.program_id(0) == 0)
    def _():
        y_ref[...] = jnp.zeros_like(y_ref)

    y_ref[...] += part * scale


def second_and_third(side, mine, other, w, b, third):
    rows, depth = mine[0].shape
    outs = third.shape[0]
    step = min(TILE, w.shape[1])
    whole = pl.BlockSpec((rows, depth), lambda i, side: (0, 0))
    return pl.pallas_call(
        functools.partial(second_kernel, w.shape[0] ** (-0.5)),
        grid_spec=pltpu.PrefetchScalarGridSpec(
            num_scalar_prefetch=1,
            grid=(w.shape[1] // step,),
            in_specs=[whole] * 4
            + [
                pl.BlockSpec((depth, step), lambda i, side: (2 * side[0], i)),
                pl.BlockSpec((depth, step), lambda i, side: (2 * side[0] + 1, i)),
                pl.BlockSpec((depth, step), lambda i, side: (2 - 2 * side[0], i)),
                pl.BlockSpec((depth, step), lambda i, side: (3 - 2 * side[0], i)),
                pl.BlockSpec((1, step), lambda i, side: (0, i)),
                pl.BlockSpec((outs, step), lambda i, side: (0, i)),
            ],
            out_specs=pl.BlockSpec((outs, rows), lambda i, side: (0, 0)),
        ),
        out_shape=jax.ShapeDtypeStruct((outs, rows), jnp.float32),
        compiler_params=pltpu.CompilerParams(vmem_limit_bytes=32 << 20),
        cost_estimate=LIGHT,
    )(side[None], *mine, *other, w, w, w, w, b, third)


def exchange(x):
    return lax.all_to_all(x, "member", split_axis=0, concat_axis=0, tiled=True)


def swap(x, axis, bit):
    count = lax.axis_size(axis)
    return lax.ppermute(x, axis, [(i, i ^ bit) for i in range(count)])


def reorder(gain_tr, order):
    pick = (order[None, :] == jnp.arange(gain_tr.shape[1])[:, None]).astype(jnp.bfloat16)
    return jnp.dot(gain_tr, pick, preferred_element_type=jnp.float32).astype(jnp.bfloat16)


def pick(x, at, axis=0):
    return lax.dynamic_index_in_dim(x, at, axis, keepdims=False)


def after(value, earlier):
    return lax.optimization_barrier((value, earlier))[0]


def body(samples, w_first, b_first, w_second, b_second, w_third, observed, perturb, variance):
    members = lax.axis_size("member")
    me = lax.axis_index("member")
    side = lax.axis_index("pair")
    width = w_first.shape[2]
    first_w, second_w, third_w = w_first[0], w_second[0], w_third[0]
    slabs_first = first_w.reshape(members, -1, width)
    slabs_second = second_w.reshape(members, -1, width)
    outs = third_w.shape[1]
    fast = members == PLANE * PLANE and width % TILE == 0
    planes = members // PLANE
    plane, place = me // PLANE, me % PLANE

    def across(x, flip):
        return swap(x, "member", flip * PLANE)

    first = [first_layer(samples, first_w, b_first, i) for i in range(2)]
    other = [swap(x, "pair", 1) for x in first]
    partial_out = second_and_third(side, first, other, second_w, b_second, third_w.T)

    half = partial_out.shape[1] // 2
    start = side * half
    keep = lax.dynamic_slice_in_dim(partial_out, start, half, 1)
    give = lax.dynamic_slice_in_dim(partial_out, (1 - side) * half, half, 1)
    pred = keep + swap(give, "pair", 1)
    observed_half = lax.dynamic_slice_in_dim(observed.T, start, half, 1)
    variance_half = lax.dynamic_slice_in_dim(variance.T, start, half, 1)
    perturb_half = lax.dynamic_slice_in_dim(perturb[0].T, start, half, 1)
    resid = observed_half + jnp.sqrt(variance_half) * perturb_half - pred
    count = pred.size // members
    both = jnp.concatenate(
        [pred.reshape(members, 1, count), resid.reshape(members, 1, count)], axis=1
    )
    got_first = exchange(slabs_first)
    var_part = lax.dynamic_index_in_dim(variance_half.reshape(members, count), me, 0)
    if fast:
        both = both.reshape((planes, PLANE) + both.shape[1:])
        parts = [pick(both, plane ^ i) for i in range(planes)]
        parts = jnp.stack([parts[0]] + [across(parts[i], i) for i in range(1, planes)])
        pad = jnp.zeros((-(outs + 2) % 8, width), jnp.bfloat16)
        small = jnp.concatenate([third_w.T, b_first, b_second, pad], axis=0)[None]
        held = [small, swap(after(small, both), "member", 8)]
        slabs_second, parts, held[1], got_first = lax.optimization_barrier(
            (slabs_second, parts, held[1], got_first)
        )
        got_second = exchange(slabs_second)
        held.append(swap(jnp.concatenate(held, axis=0), "member", 4))
        both = jnp.stack([pick(parts, plane ^ i) for i in range(planes)])
        parts = [pick(both, place ^ i, 1) for i in range(PLANE)]
        parts = jnp.stack([parts[0]] + [swap(parts[i], "member", i) for i in range(1, PLANE)])
        both = jnp.stack([pick(parts, place ^ i) for i in range(PLANE)], axis=1)
        both = both.reshape((members,) + both.shape[2:])
        sums = whole_call(
            moments_kernel,
            jax.ShapeDtypeStruct((members, 2 * members), jnp.float32),
            both,
            var_part,
        )
        sums = sums + swap(sums, "pair", 1)
        sums = sums + swap(sums, "member", 1)
        sums = sums + swap(sums, "member", 2)
        held[2] = after(held[2], sums)
        held.append(swap(jnp.concatenate(held, axis=0), "member", 2))
        far = [across(sums, i) for i in range(1, planes)]
        gain, spread, mixed_second = solve([sums] + far, got_second)
        mixed_second, got_first, held[3] = lax.optimization_barrier(
            (mixed_second, got_first, held[3])
        )
        new_second = exchange(mixed_second)

        mixed_first = blocked(mix_kernel, got_first, spread)
        mixed_first = mixed_first.reshape((planes, PLANE) + mixed_first.shape[1:])
        parts = [pick(mixed_first, place ^ i, 1) for i in range(PLANE)]
        parts = jnp.stack([parts[0]] + [swap(parts[i], "member", i) for i in range(1, PLANE)])
        held[3] = after(held[3], parts)
        held.append(swap(jnp.concatenate(held, axis=0), "member", 1))
        homes = []
        for flip in range(planes):
            block = jnp.stack([pick(pick(parts, place ^ i), plane ^ flip) for i in range(PLANE)])
            homes.append(across(block, flip) if flip else block)

        order = me[None]
        for bit in (8, 4, 2, 1):
            order = jnp.concatenate([order, order ^ bit])
        column = reorder(pick(gain, me, 1)[None], order)[0].astype(jnp.float32)
        new_small = mix_one(column, held)
        new_third = new_small[:outs].T
        new_bfirst = new_small[outs : outs + 1]
        new_bsecond = new_small[outs + 1 : outs + 2]
        new_second = blocked(copy_kernel, new_second)
        homes, new_second, new_third, new_bfirst, new_bsecond = lax.optimization_barrier(
            (homes, new_second, new_third, new_bfirst, new_bsecond)
        )
        new_first = jnp.zeros(slabs_first.shape, jnp.bfloat16)
        for flip, part in enumerate(homes):
            new_first = lax.dynamic_update_slice_in_dim(
                new_first, part, (plane ^ flip) * PLANE, 0
            )
    else:
        both = exchange(both)
        allpred, allres = both[:, 0], both[:, 1]
        devpred = allpred - jnp.mean(allpred, axis=0, keepdims=True)
        scaled = devpred / var_part
        sums = jnp.dot(
            scaled, jnp.concatenate([devpred, allres], axis=0).T, precision=lax.Precision.HIGHEST
        )
        sums = lax.psum(sums, ("member", "pair"))
        gain = solve_gain(sums[:, :members], sums[:, members:])
        gain_tr = gain.astype(jnp.bfloat16).T
        new_second = exchange(mix_plain(exchange(slabs_second), gain_tr))
        new_first = exchange(mix_plain(got_first, gain_tr))
        small = jnp.concatenate([third_w.T, b_first, b_second], axis=0)
        full = lax.all_gather(small, "member", axis=0)
        new_small = mix_plain(full, lax.dynamic_index_in_dim(gain_tr, me, 0))[0]
        new_third = new_small[:outs].T
        new_bfirst = new_small[outs : outs + 1]
        new_bsecond = new_small[outs + 1 :]
    return (
        new_first.reshape(w_first.shape),
        new_bfirst,
        new_second.reshape(w_second.shape),
        new_bsecond,
        new_third[None],
    )


def solution(mesh):
    in_specs = (
        P(),
        P("member", None, "pair"),
        P("member", "pair"),
        P("member", None, "pair"),
        P("member", "pair"),
        P("member", "pair", None),
        P(),
        P("member", None, None),
        P(),
    )
    out_specs = (
        P("member", None, "pair"),
        P("member", "pair"),
        P("member", None, "pair"),
        P("member", "pair"),
        P("member", "pair", None),
    )
    return jax.shard_map(body, mesh=mesh, in_specs=in_specs, out_specs=out_specs, check_vma=False)
```

```python
import functools

import jax
import jax.numpy as jnp
from jax import lax
from jax.experimental import pallas as pl
from jax.experimental.pallas import tpu as pltpu
from jax.sharding import PartitionSpec as P

ROW_BITS = 4
ROWS = 1 << ROW_BITS
PLANE = 4
TILE = 256
VMEM = 56 << 20
LIGHT = pl.CostEstimate(flops=1, bytes_accessed=1, transcendentals=0)


def solve_gain(amat, bmat):
    count = amat.shape[0]
    system = amat + count * jnp.eye(count, dtype=jnp.float32)
    factor = jnp.linalg.cholesky(system)
    middle = lax.linalg.triangular_solve(
        factor, bmat, left_side=True, lower=True, transpose_a=False
    )
    return lax.linalg.triangular_solve(factor, middle, left_side=True, lower=True, transpose_a=True)


def mix_rows(spread_ref, x_ref, y_ref, at):
    members, _, width = x_ref.shape
    for left in range(0, width, TILE):
        piece = (slice(None), pl.ds(at, ROWS), pl.ds(left, TILE))
        full = x_ref[piece].astype(jnp.float32)
        mean = jnp.sum(full, axis=0, keepdims=True) * (1.0 / members)
        center = (full - mean).astype(jnp.bfloat16).reshape(members * ROWS, TILE)
        mixed = jnp.dot(spread_ref[...], center, preferred_element_type=jnp.float32)
        y_ref[piece] = mixed.astype(jnp.bfloat16).reshape(members, ROWS, TILE)


def mix_kernel(spread_ref, x_ref, y_ref):
    for at in range(0, x_ref.shape[1], ROWS):
        mix_rows(spread_ref, x_ref, y_ref, at)


def copy_kernel(x_ref, y_ref):
    y_ref[...] = x_ref[...]


def blocked(kernel, x, *wholes):
    members, total, width = x.shape
    rows = min(total, 4 * ROWS)
    block = pl.BlockSpec((members, rows, width), lambda i: (0, i, 0))
    return pl.pallas_call(
        kernel,
        grid=(total // rows,),
        in_specs=[pl.BlockSpec(w.shape, lambda i: (0, 0)) for w in wholes] + [block],
        out_specs=block,
        out_shape=jax.ShapeDtypeStruct(x.shape, jnp.bfloat16),
        compiler_params=pltpu.CompilerParams(vmem_limit_bytes=VMEM),
        cost_estimate=LIGHT,
    )(*wholes, x)


def moments_kernel(both_ref, var_ref, sums_ref):
    pred, resid = both_ref[:, 0, :], both_ref[:, 1, :]
    dev = pred - jnp.sum(pred, axis=0, keepdims=True) * (1.0 / pred.shape[0])
    scaled = dev / var_ref[...]
    sums_ref[...] = lax.dot_general(
        scaled,
        jnp.concatenate([dev, resid], axis=0),
        (((1,), (1,)), ((), ())),
        precision=lax.Precision.HIGHEST,
        preferred_element_type=jnp.float32,
    )


def whole_call(kernel, out_shape, *args):
    return pl.pallas_call(kernel, out_shape=out_shape, cost_estimate=LIGHT)(*args)


def solve_kernel(
    own_ref, far1_ref, far2_ref, far3_ref, x_ref, gain_ref, spread_ref, y_ref, x_buf, y_buf, x_sem, y_sems
):
    load = pltpu.make_async_copy(x_ref, x_buf, x_sem)
    load.start()
    total = (own_ref[...] + far1_ref[...]) + (far2_ref[...] + far3_ref[...])
    count = total.shape[0]
    row = lax.broadcasted_iota(jnp.int32, total.shape, 0)
    col = lax.broadcasted_iota(jnp.int32, total.shape, 1)
    total = total + jnp.where(row == col, float(count), 0.0)
    for k in range(count):
        pivot = total[k : k + 1, :] / total[k : k + 1, k : k + 1]
        factor = jnp.where(row == k, total - 1.0, total)[:, k : k + 1]
        total = total - factor * pivot
    gain = total[:, count:].astype(jnp.bfloat16)
    gain_ref[...] = gain
    size = count * ROWS
    row = lax.broadcasted_iota(jnp.int32, (size, count), 0)
    col = lax.broadcasted_iota(jnp.int32, (size, count), 1)
    expand = (row >> ROW_BITS == col).astype(jnp.bfloat16)
    wide = lax.dot_general(
        expand, gain, (((1,), (1,)), ((), ())), preferred_element_type=jnp.float32
    ).astype(jnp.bfloat16)
    wide = lax.dot_general(
        wide, expand, (((1,), (1,)), ((), ())), preferred_element_type=jnp.float32
    )
    at_row = lax.broadcasted_iota(jnp.int32, (size, size), 0)
    at_col = lax.broadcasted_iota(jnp.int32, (size, size), 1)
    same = ((at_row ^ at_col) & (ROWS - 1)) == 0
    spread_ref[...] = jnp.where(same, wide, 0.0).astype(jnp.bfloat16)

    load.wait()
    stores = []
    for i in range(x_ref.shape[1] // ROWS):
        rows = (slice(None), pl.ds(i * ROWS, ROWS), slice(None))
        mix_rows(spread_ref, x_buf, y_buf, i * ROWS)
        stores.append(pltpu.make_async_copy(y_buf.at[rows], y_ref.at[rows], y_sems.at[i]))
        stores[-1].start()
    for store in stores:
        store.wait()


def solve(sums, x):
    members = x.shape[0]
    size = members * ROWS
    vmem, anywhere = pl.BlockSpec(memory_space=pltpu.VMEM), pl.BlockSpec(memory_space=pl.ANY)
    return pl.pallas_call(
        solve_kernel,
        in_specs=[vmem] * len(sums) + [anywhere],
        out_specs=[vmem, vmem, anywhere],
        out_shape=[
            jax.ShapeDtypeStruct((members, members), jnp.bfloat16),
            jax.ShapeDtypeStruct((size, size), jnp.bfloat16),
            jax.ShapeDtypeStruct(x.shape, x.dtype),
        ],
        scratch_shapes=[
            pltpu.VMEM(x.shape, x.dtype),
            pltpu.VMEM(x.shape, x.dtype),
            pltpu.SemaphoreType.DMA,
            pltpu.SemaphoreType.DMA((x.shape[1] // ROWS,)),
        ],
        compiler_params=pltpu.CompilerParams(vmem_limit_bytes=VMEM),
        cost_estimate=LIGHT,
    )(*sums, x)


def mix_plain(slab, gain_tr):
    full = slab.astype(jnp.float32)
    center = (full - jnp.mean(full, axis=0, keepdims=True)).astype(jnp.bfloat16)
    return jnp.einsum(
        "jk,krc->jrc", gain_tr, center, preferred_element_type=jnp.float32
    ).astype(jnp.bfloat16)


def mix_one(column, blocks):
    full = [block.astype(jnp.float32) for block in blocks]
    mean = sum(jnp.sum(block, axis=0) for block in full) * (1.0 / column.shape[0])
    total = jnp.zeros_like(mean)
    at = 0
    for block in full:
        count = block.shape[0]
        center = (block - mean).astype(jnp.bfloat16).astype(jnp.float32)
        total = total + jnp.sum(center * column[at : at + count, None, None], axis=0)
        at += count
    return total.astype(jnp.bfloat16)


def first_kernel(scale, x_ref, w_ref, b_ref, y_ref):
    summed = jnp.dot(x_ref[...], w_ref[...], preferred_element_type=jnp.float32)
    y = jax.nn.gelu(summed * scale + b_ref[...].astype(jnp.float32), approximate=True)
    y_ref[...] = y.astype(jnp.bfloat16)


def first_layer(x, w, b, part):
    rows, depth = x.shape
    half = w.shape[1] // 2
    step = min(TILE, half)
    first = part * (half // step)
    return pl.pallas_call(
        functools.partial(first_kernel, depth ** (-0.5)),
        grid=(half // step,),
        in_specs=[
            pl.BlockSpec((rows, depth), lambda i: (0, 0)),
            pl.BlockSpec((depth, step), lambda i: (0, i + first)),
            pl.BlockSpec((1, step), lambda i: (0, i + first)),
        ],
        out_specs=pl.BlockSpec((rows, step), lambda i: (0, i)),
        out_shape=jax.ShapeDtypeStruct((rows, half), jnp.bfloat16),
        compiler_params=pltpu.CompilerParams(vmem_limit_bytes=32 << 20),
        cost_estimate=LIGHT,
    )(x, w, b)


def second_kernel(scale, side_ref, *refs):
    inputs, weights, (b_ref, third_ref, y_ref) = refs[:4], refs[4:8], refs[8:]
    summed = sum(
        jnp.dot(x_ref[...], w_ref[...], preferred_element_type=jnp.float32)
        for x_ref, w_ref in zip(inputs, weights)
    )
    y = jax.nn.gelu(summed * scale + b_ref[...].astype(jnp.float32), approximate=True)
    part = lax.dot_general(
        third_ref[...],
        y.astype(jnp.bfloat16),
        (((1,), (1,)), ((), ())),
        preferred_element_type=jnp.float32,
    )

    @pl.when(pl.program_id(0) == 0)
    def _():
        y_ref[...] = jnp.zeros_like(y_ref)

    y_ref[...] += part * scale


def second_and_third(side, mine, other, w, b, third):
    rows, depth = mine[0].shape
    outs = third.shape[0]
    step = min(TILE, w.shape[1])
    whole = pl.BlockSpec((rows, depth), lambda i, side: (0, 0))
    return pl.pallas_call(
        functools.partial(second_kernel, w.shape[0] ** (-0.5)),
        grid_spec=pltpu.PrefetchScalarGridSpec(
            num_scalar_prefetch=1,
            grid=(w.shape[1] // step,),
            in_specs=[whole] * 4
            + [
                pl.BlockSpec((depth, step), lambda i, side: (2 * side[0], i)),
                pl.BlockSpec((depth, step), lambda i, side: (2 * side[0] + 1, i)),
                pl.BlockSpec((depth, step), lambda i, side: (2 - 2 * side[0], i)),
                pl.BlockSpec((depth, step), lambda i, side: (3 - 2 * side[0], i)),
                pl.BlockSpec((1, step), lambda i, side: (0, i)),
                pl.BlockSpec((outs, step), lambda i, side: (0, i)),
            ],
            out_specs=pl.BlockSpec((outs, rows), lambda i, side: (0, 0)),
        ),
        out_shape=jax.ShapeDtypeStruct((outs, rows), jnp.float32),
        compiler_params=pltpu.CompilerParams(vmem_limit_bytes=32 << 20),
        cost_estimate=LIGHT,
    )(side[None], *mine, *other, w, w, w, w, b, third)


def exchange(x):
    return lax.all_to_all(x, "member", split_axis=0, concat_axis=0, tiled=True)


def swap(x, axis, bit):
    count = lax.axis_size(axis)
    return lax.ppermute(x, axis, [(i, i ^ bit) for i in range(count)])


def reorder(gain_tr, order):
    pick = (order[None, :] == jnp.arange(gain_tr.shape[1])[:, None]).astype(jnp.bfloat16)
    return jnp.dot(gain_tr, pick, preferred_element_type=jnp.float32).astype(jnp.bfloat16)


def pick(x, at, axis=0):
    return lax.dynamic_index_in_dim(x, at, axis, keepdims=False)


def after(value, earlier):
    return lax.optimization_barrier((value, earlier))[0]


def body(samples, w_first, b_first, w_second, b_second, w_third, observed, perturb, variance):
    members = lax.axis_size("member")
    me = lax.axis_index("member")
    side = lax.axis_index("pair")
    width = w_first.shape[2]
    first_w, second_w, third_w = w_first[0], w_second[0], w_third[0]
    slabs_first = first_w.reshape(members, -1, width)
    slabs_second = second_w.reshape(members, -1, width)
    outs = third_w.shape[1]
    fast = members == PLANE * PLANE and width % TILE == 0
    planes = members // PLANE
    plane, place = me // PLANE, me % PLANE

    def across(x, flip):
        return swap(x, "member", flip * PLANE)

    first = [first_layer(samples, first_w, b_first, i) for i in range(2)]
    other = [swap(x, "pair", 1) for x in first]
    partial_out = second_and_third(side, first, other, second_w, b_second, third_w.T)

    half = partial_out.shape[1] // 2
    start = side * half
    keep = lax.dynamic_slice_in_dim(partial_out, start, half, 1)
    give = lax.dynamic_slice_in_dim(partial_out, (1 - side) * half, half, 1)
    pred = keep + swap(give, "pair", 1)
    observed_half = lax.dynamic_slice_in_dim(observed.T, start, half, 1)
    variance_half = lax.dynamic_slice_in_dim(variance.T, start, half, 1)
    perturb_half = lax.dynamic_slice_in_dim(perturb[0].T, start, half, 1)
    resid = observed_half + jnp.sqrt(variance_half) * perturb_half - pred
    count = pred.size // members
    both = jnp.concatenate(
        [pred.reshape(members, 1, count), resid.reshape(members, 1, count)], axis=1
    )
    got_first = exchange(slabs_first)
    var_part = lax.dynamic_index_in_dim(variance_half.reshape(members, count), me, 0)
    if fast:
        both = both.reshape((planes, PLANE) + both.shape[1:])
        parts = [pick(both, plane ^ i) for i in range(planes)]
        parts = jnp.stack([parts[0]] + [across(parts[i], i) for i in range(1, planes)])
        small = jnp.concatenate([third_w.T, b_first, b_second], axis=0)[None]
        held = [small, swap(after(small, both), "member", 8)]
        slabs_second, parts, held[1], got_first = lax.optimization_barrier(
            (slabs_second, parts, held[1], got_first)
        )
        got_second = exchange(slabs_second)
        held.append(swap(jnp.concatenate(held, axis=0), "member", 4))
        both = jnp.stack([pick(parts, plane ^ i) for i in range(planes)])
        parts = [pick(both, place ^ i, 1) for i in range(PLANE)]
        parts = jnp.stack([parts[0]] + [swap(parts[i], "member", i) for i in range(1, PLANE)])
        both = jnp.stack([pick(parts, place ^ i) for i in range(PLANE)], axis=1)
        both = both.reshape((members,) + both.shape[2:])
        sums = whole_call(
            moments_kernel,
            jax.ShapeDtypeStruct((members, 2 * members), jnp.float32),
            both,
            var_part,
        )
        sums = sums + swap(sums, "pair", 1)
        sums = sums + swap(sums, "member", 1)
        sums = sums + swap(sums, "member", 2)
        held[2] = after(held[2], sums)
        held.append(swap(jnp.concatenate(held, axis=0), "member", 2))
        far = [across(sums, i) for i in range(1, planes)]
        gain, spread, mixed_second = solve([sums] + far, got_second)
        mixed_second, got_first, held[3] = lax.optimization_barrier(
            (mixed_second, got_first, held[3])
        )
        new_second = exchange(mixed_second)

        mixed_first = blocked(mix_kernel, got_first, spread)
        mixed_first = mixed_first.reshape((planes, PLANE) + mixed_first.shape[1:])
        parts = [pick(mixed_first, place ^ i, 1) for i in range(PLANE)]
        parts = jnp.stack([parts[0]] + [swap(parts[i], "member", i) for i in range(1, PLANE)])
        held[3] = after(held[3], parts)
        held.append(swap(jnp.concatenate(held, axis=0), "member", 1))
        homes = []
        for flip in range(planes):
            block = jnp.stack([pick(pick(parts, place ^ i), plane ^ flip) for i in range(PLANE)])
            homes.append(across(block, flip) if flip else block)

        order = me[None]
        for bit in (8, 4, 2, 1):
            order = jnp.concatenate([order, order ^ bit])
        column = reorder(pick(gain, me, 1)[None], order)[0].astype(jnp.float32)
        new_small = mix_one(column, held)
        new_third = new_small[:outs].T
        new_bfirst = new_small[outs : outs + 1]
        new_bsecond = new_small[outs + 1 : outs + 2]
        new_second = blocked(copy_kernel, new_second)
        homes, new_second, new_third, new_bfirst, new_bsecond = lax.optimization_barrier(
            (homes, new_second, new_third, new_bfirst, new_bsecond)
        )
        new_first = jnp.zeros(slabs_first.shape, jnp.bfloat16)
        for flip, part in enumerate(homes):
            new_first = lax.dynamic_update_slice_in_dim(
                new_first, part, (plane ^ flip) * PLANE, 0
            )
    else:
        both = exchange(both)
        allpred, allres = both[:, 0], both[:, 1]
        devpred = allpred - jnp.mean(allpred, axis=0, keepdims=True)
        scaled = devpred / var_part
        sums = jnp.dot(
            scaled, jnp.concatenate([devpred, allres], axis=0).T, precision=lax.Precision.HIGHEST
        )
        sums = lax.psum(sums, ("member", "pair"))
        gain = solve_gain(sums[:, :members], sums[:, members:])
        gain_tr = gain.astype(jnp.bfloat16).T
        new_second = exchange(mix_plain(exchange(slabs_second), gain_tr))
        new_first = exchange(mix_plain(got_first, gain_tr))
        small = jnp.concatenate([third_w.T, b_first, b_second], axis=0)
        full = lax.all_gather(small, "member", axis=0)
        new_small = mix_plain(full, lax.dynamic_index_in_dim(gain_tr, me, 0))[0]
        new_third = new_small[:outs].T
        new_bfirst = new_small[outs : outs + 1]
        new_bsecond = new_small[outs + 1 :]
    return (
        new_first.reshape(w_first.shape),
        new_bfirst,
        new_second.reshape(w_second.shape),
        new_bsecond,
        new_third[None],
    )


def solution(mesh):
    in_specs = (
        P(),
        P("member", None, "pair"),
        P("member", "pair"),
        P("member", None, "pair"),
        P("member", "pair"),
        P("member", "pair", None),
        P(),
        P("member", None, None),
        P(),
    )
    out_specs = (
        P("member", None, "pair"),
        P("member", "pair"),
        P("member", None, "pair"),
        P("member", "pair"),
        P("member", "pair", None),
    )
    return jax.shard_map(body, mesh=mesh, in_specs=in_specs, out_specs=out_specs, check_vma=False)
```

```python
import functools

import jax
import jax.numpy as jnp
from jax import lax
from jax.experimental import pallas as pl
from jax.experimental.pallas import tpu as pltpu
from jax.sharding import PartitionSpec as P

ROW_BITS = 4
ROWS = 1 << ROW_BITS
PLANE = 4
TILE = 256
VMEM = 56 << 20
LIGHT = pl.CostEstimate(flops=1, bytes_accessed=1, transcendentals=0)


def solve_gain(amat, bmat):
    count = amat.shape[0]
    system = amat + count * jnp.eye(count, dtype=jnp.float32)
    factor = jnp.linalg.cholesky(system)
    middle = lax.linalg.triangular_solve(
        factor, bmat, left_side=True, lower=True, transpose_a=False
    )
    return lax.linalg.triangular_solve(factor, middle, left_side=True, lower=True, transpose_a=True)


def mix_rows(spread_ref, x_ref, y_ref, at):
    members, _, width = x_ref.shape
    for left in range(0, width, TILE):
        piece = (slice(None), pl.ds(at, ROWS), pl.ds(left, TILE))
        full = x_ref[piece].astype(jnp.float32)
        mean = jnp.sum(full, axis=0, keepdims=True) * (1.0 / members)
        center = (full - mean).astype(jnp.bfloat16).reshape(members * ROWS, TILE)
        mixed = jnp.dot(spread_ref[...], center, preferred_element_type=jnp.float32)
        y_ref[piece] = mixed.astype(jnp.bfloat16).reshape(members, ROWS, TILE)


def center_kernel(x_ref, y_ref):
    members, rows, width = x_ref.shape
    for at in range(0, rows, ROWS):
        for left in range(0, width, TILE):
            piece = (slice(None), pl.ds(at, ROWS), pl.ds(left, TILE))
            full = x_ref[piece].astype(jnp.float32)
            mean = jnp.sum(full, axis=0, keepdims=True) * (1.0 / members)
            y_ref[piece] = (full - mean).astype(jnp.bfloat16)


def apply_rows(spread_ref, x_ref, y_ref, at):
    members, _, width = x_ref.shape
    rows = (slice(None), pl.ds(at, ROWS), slice(None))
    center = x_ref[rows].reshape(members * ROWS, width)
    mixed = jnp.dot(spread_ref[...], center, preferred_element_type=jnp.float32)
    y_ref[rows] = mixed.astype(jnp.bfloat16).reshape(members, ROWS, width)


def mix_kernel(spread_ref, x_ref, y_ref):
    for at in range(0, x_ref.shape[1], ROWS):
        mix_rows(spread_ref, x_ref, y_ref, at)


def copy_kernel(x_ref, y_ref):
    y_ref[...] = x_ref[...]


def blocked(kernel, x, *wholes):
    members, total, width = x.shape
    rows = min(total, 4 * ROWS)
    block = pl.BlockSpec((members, rows, width), lambda i: (0, i, 0))
    return pl.pallas_call(
        kernel,
        grid=(total // rows,),
        in_specs=[pl.BlockSpec(w.shape, lambda i: (0, 0)) for w in wholes] + [block],
        out_specs=block,
        out_shape=jax.ShapeDtypeStruct(x.shape, jnp.bfloat16),
        compiler_params=pltpu.CompilerParams(vmem_limit_bytes=VMEM),
        cost_estimate=LIGHT,
    )(*wholes, x)


def moments_kernel(both_ref, var_ref, sums_ref):
    pred, resid = both_ref[:, 0, :], both_ref[:, 1, :]
    dev = pred - jnp.sum(pred, axis=0, keepdims=True) * (1.0 / pred.shape[0])
    scaled = dev / var_ref[...]
    sums_ref[...] = lax.dot_general(
        scaled,
        jnp.concatenate([dev, resid], axis=0),
        (((1,), (1,)), ((), ())),
        precision=lax.Precision.HIGHEST,
        preferred_element_type=jnp.float32,
    )


def whole_call(kernel, out_shape, *args):
    return pl.pallas_call(kernel, out_shape=out_shape, cost_estimate=LIGHT)(*args)


def solve_kernel(
    own_ref, far1_ref, far2_ref, far3_ref, x_ref, gain_ref, spread_ref, y_ref, x_buf, y_buf, x_sem, y_sems
):
    load = pltpu.make_async_copy(x_ref, x_buf, x_sem)
    load.start()
    total = (own_ref[...] + far1_ref[...]) + (far2_ref[...] + far3_ref[...])
    count = total.shape[0]
    row = lax.broadcasted_iota(jnp.int32, total.shape, 0)
    col = lax.broadcasted_iota(jnp.int32, total.shape, 1)
    total = total + jnp.where(row == col, float(count), 0.0)
    for k in range(count):
        pivot = total[k : k + 1, :] / total[k : k + 1, k : k + 1]
        factor = jnp.where(row == k, total - 1.0, total)[:, k : k + 1]
        total = total - factor * pivot
    gain = total[:, count:].astype(jnp.bfloat16)
    gain_ref[...] = gain
    size = count * ROWS
    row = lax.broadcasted_iota(jnp.int32, (size, count), 0)
    col = lax.broadcasted_iota(jnp.int32, (size, count), 1)
    expand = (row >> ROW_BITS == col).astype(jnp.bfloat16)
    wide = lax.dot_general(
        expand, gain, (((1,), (1,)), ((), ())), preferred_element_type=jnp.float32
    ).astype(jnp.bfloat16)
    wide = lax.dot_general(
        wide, expand, (((1,), (1,)), ((), ())), preferred_element_type=jnp.float32
    )
    at_row = lax.broadcasted_iota(jnp.int32, (size, size), 0)
    at_col = lax.broadcasted_iota(jnp.int32, (size, size), 1)
    same = ((at_row ^ at_col) & (ROWS - 1)) == 0
    spread_ref[...] = jnp.where(same, wide, 0.0).astype(jnp.bfloat16)

    load.wait()
    stores = []
    for i in range(x_ref.shape[1] // ROWS):
        rows = (slice(None), pl.ds(i * ROWS, ROWS), slice(None))
        apply_rows(spread_ref, x_buf, y_buf, i * ROWS)
        stores.append(pltpu.make_async_copy(y_buf.at[rows], y_ref.at[rows], y_sems.at[i]))
        stores[-1].start()
    for store in stores:
        store.wait()


def solve(sums, x):
    members = x.shape[0]
    size = members * ROWS
    vmem, anywhere = pl.BlockSpec(memory_space=pltpu.VMEM), pl.BlockSpec(memory_space=pl.ANY)
    return pl.pallas_call(
        solve_kernel,
        in_specs=[vmem] * len(sums) + [anywhere],
        out_specs=[vmem, vmem, anywhere],
        out_shape=[
            jax.ShapeDtypeStruct((members, members), jnp.bfloat16),
            jax.ShapeDtypeStruct((size, size), jnp.bfloat16),
            jax.ShapeDtypeStruct(x.shape, x.dtype),
        ],
        scratch_shapes=[
            pltpu.VMEM(x.shape, x.dtype),
            pltpu.VMEM(x.shape, x.dtype),
            pltpu.SemaphoreType.DMA,
            pltpu.SemaphoreType.DMA((x.shape[1] // ROWS,)),
        ],
        compiler_params=pltpu.CompilerParams(vmem_limit_bytes=VMEM),
        cost_estimate=LIGHT,
    )(*sums, x)


def mix_plain(slab, gain_tr):
    full = slab.astype(jnp.float32)
    center = (full - jnp.mean(full, axis=0, keepdims=True)).astype(jnp.bfloat16)
    return jnp.einsum(
        "jk,krc->jrc", gain_tr, center, preferred_element_type=jnp.float32
    ).astype(jnp.bfloat16)


def mix_one(column, blocks):
    full = [block.astype(jnp.float32) for block in blocks]
    mean = sum(jnp.sum(block, axis=0) for block in full) * (1.0 / column.shape[0])
    total = jnp.zeros_like(mean)
    at = 0
    for block in full:
        count = block.shape[0]
        center = (block - mean).astype(jnp.bfloat16).astype(jnp.float32)
        total = total + jnp.sum(center * column[at : at + count, None, None], axis=0)
        at += count
    return total.astype(jnp.bfloat16)


def place_kernel(at_ref, *refs):
    parts, out_ref, sems = refs[:-2], refs[-2], refs[-1]
    size = parts[0].shape[0]
    copies = [
        pltpu.make_async_copy(
            part, out_ref.at[pl.ds((at_ref[0] ^ flip) * size, size)], sems.at[flip]
        )
        for flip, part in enumerate(parts)
    ]
    for copy in copies:
        copy.start()
    for copy in copies:
        copy.wait()


def place_parts(at, parts):
    count, shape = len(parts), parts[0].shape
    return pl.pallas_call(
        place_kernel,
        in_specs=[pl.BlockSpec(memory_space=pltpu.SMEM)]
        + [pl.BlockSpec(memory_space=pltpu.VMEM)] * count,
        out_specs=pl.BlockSpec(memory_space=pl.ANY),
        out_shape=jax.ShapeDtypeStruct((count * shape[0],) + shape[1:], parts[0].dtype),
        scratch_shapes=[pltpu.SemaphoreType.DMA((count,))],
        compiler_params=pltpu.CompilerParams(vmem_limit_bytes=32 << 20),
        cost_estimate=LIGHT,
    )(at[None], *parts)


def first_kernel(scale, x_ref, w_ref, b_ref, y_ref):
    summed = jnp.dot(x_ref[...], w_ref[...], preferred_element_type=jnp.float32)
    y = jax.nn.gelu(summed * scale + b_ref[...].astype(jnp.float32), approximate=True)
    y_ref[...] = y.astype(jnp.bfloat16)


def first_layer(x, w, b, part):
    rows, depth = x.shape
    half = w.shape[1] // 2
    step = min(TILE, half)
    first = part * (half // step)
    return pl.pallas_call(
        functools.partial(first_kernel, depth ** (-0.5)),
        grid=(half // step,),
        in_specs=[
            pl.BlockSpec((rows, depth), lambda i: (0, 0)),
            pl.BlockSpec((depth, step), lambda i: (0, i + first)),
            pl.BlockSpec((1, step), lambda i: (0, i + first)),
        ],
        out_specs=pl.BlockSpec((rows, step), lambda i: (0, i)),
        out_shape=jax.ShapeDtypeStruct((rows, half), jnp.bfloat16),
        compiler_params=pltpu.CompilerParams(vmem_limit_bytes=32 << 20),
        cost_estimate=LIGHT,
    )(x, w, b)


def second_kernel(scale, side_ref, *refs):
    inputs, weights, (b_ref, third_ref, y_ref) = refs[:4], refs[4:8], refs[8:]
    summed = sum(
        jnp.dot(x_ref[...], w_ref[...], preferred_element_type=jnp.float32)
        for x_ref, w_ref in zip(inputs, weights)
    )
    y = jax.nn.gelu(summed * scale + b_ref[...].astype(jnp.float32), approximate=True)
    part = lax.dot_general(
        third_ref[...],
        y.astype(jnp.bfloat16),
        (((1,), (1,)), ((), ())),
        preferred_element_type=jnp.float32,
    )

    @pl.when(pl.program_id(0) == 0)
    def _():
        y_ref[...] = jnp.zeros_like(y_ref)

    y_ref[...] += part * scale


def second_and_third(side, mine, other, w, b, third):
    rows, depth = mine[0].shape
    outs = third.shape[0]
    step = min(TILE, w.shape[1])
    whole = pl.BlockSpec((rows, depth), lambda i, side: (0, 0))
    return pl.pallas_call(
        functools.partial(second_kernel, w.shape[0] ** (-0.5)),
        grid_spec=pltpu.PrefetchScalarGridSpec(
            num_scalar_prefetch=1,
            grid=(w.shape[1] // step,),
            in_specs=[whole] * 4
            + [
                pl.BlockSpec((depth, step), lambda i, side: (2 * side[0], i)),
                pl.BlockSpec((depth, step), lambda i, side: (2 * side[0] + 1, i)),
                pl.BlockSpec((depth, step), lambda i, side: (2 - 2 * side[0], i)),
                pl.BlockSpec((depth, step), lambda i, side: (3 - 2 * side[0], i)),
                pl.BlockSpec((1, step), lambda i, side: (0, i)),
                pl.BlockSpec((outs, step), lambda i, side: (0, i)),
            ],
            out_specs=pl.BlockSpec((outs, rows), lambda i, side: (0, 0)),
        ),
        out_shape=jax.ShapeDtypeStruct((outs, rows), jnp.float32),
        compiler_params=pltpu.CompilerParams(vmem_limit_bytes=32 << 20),
        cost_estimate=LIGHT,
    )(side[None], *mine, *other, w, w, w, w, b, third)


def exchange(x):
    return lax.all_to_all(x, "member", split_axis=0, concat_axis=0, tiled=True)


def swap(x, axis, bit):
    count = lax.axis_size(axis)
    return lax.ppermute(x, axis, [(i, i ^ bit) for i in range(count)])


def reorder(gain_tr, order):
    pick = (order[None, :] == jnp.arange(gain_tr.shape[1])[:, None]).astype(jnp.bfloat16)
    return jnp.dot(gain_tr, pick, preferred_element_type=jnp.float32).astype(jnp.bfloat16)


def pick(x, at, axis=0):
    return lax.dynamic_index_in_dim(x, at, axis, keepdims=False)


def after(value, earlier):
    return lax.optimization_barrier((value, earlier))[0]


def body(samples, w_first, b_first, w_second, b_second, w_third, observed, perturb, variance):
    members = lax.axis_size("member")
    me = lax.axis_index("member")
    side = lax.axis_index("pair")
    width = w_first.shape[2]
    first_w, second_w, third_w = w_first[0], w_second[0], w_third[0]
    slabs_first = first_w.reshape(members, -1, width)
    slabs_second = second_w.reshape(members, -1, width)
    outs = third_w.shape[1]
    fast = members == PLANE * PLANE and width % TILE == 0
    planes = members // PLANE
    plane, place = me // PLANE, me % PLANE

    def across(x, flip):
        return swap(x, "member", flip * PLANE)

    first = [first_layer(samples, first_w, b_first, i) for i in range(2)]
    other = [swap(x, "pair", 1) for x in first]
    partial_out = second_and_third(side, first, other, second_w, b_second, third_w.T)

    half = partial_out.shape[1] // 2
    start = side * half
    keep = lax.dynamic_slice_in_dim(partial_out, start, half, 1)
    give = lax.dynamic_slice_in_dim(partial_out, (1 - side) * half, half, 1)
    pred = keep + swap(give, "pair", 1)
    observed_half = lax.dynamic_slice_in_dim(observed.T, start, half, 1)
    variance_half = lax.dynamic_slice_in_dim(variance.T, start, half, 1)
    perturb_half = lax.dynamic_slice_in_dim(perturb[0].T, start, half, 1)
    resid = observed_half + jnp.sqrt(variance_half) * perturb_half - pred
    count = pred.size // members
    both = jnp.concatenate(
        [pred.reshape(members, 1, count), resid.reshape(members, 1, count)], axis=1
    )
    got_second = exchange(slabs_second)
    var_part = lax.dynamic_index_in_dim(variance_half.reshape(members, count), me, 0)
    if fast:
        def by_plane(parts):
            parts = jnp.stack(parts)
            return jnp.stack([pick(parts, plane ^ i) for i in range(planes)])

        def within(x):
            parts = [pick(x, place ^ i, 1) for i in range(PLANE)]
            parts = jnp.stack([parts[0]] + [swap(parts[i], "member", i) for i in range(1, PLANE)])
            return jnp.stack([pick(parts, place ^ i) for i in range(PLANE)])

        slabs = within(slabs_first.reshape((planes, PLANE) + slabs_first.shape[1:]))
        both, slabs = lax.optimization_barrier((both, slabs))
        both = within(both.reshape((planes, PLANE) + both.shape[1:]))
        parts = [pick(both, plane ^ i, 1) for i in range(planes)]
        parts = [parts[0]] + [across(parts[i], i) for i in range(1, planes)]
        parts, slabs = lax.optimization_barrier((parts, slabs))
        both = jnp.concatenate(by_plane(parts), axis=0)
        parts = [pick(slabs, plane ^ i, 1) for i in range(planes)]
        parts = [parts[0]] + [across(parts[i], i) for i in range(1, planes)]
        sums = whole_call(
            moments_kernel,
            jax.ShapeDtypeStruct((members, 2 * members), jnp.float32),
            both,
            var_part,
        )
        sums = sums + swap(sums, "pair", 1)
        sums = sums + swap(sums, "member", 1)
        sums = sums + swap(sums, "member", 2)
        small = jnp.concatenate([third_w.T, b_first, b_second], axis=0)[None]
        center = blocked(center_kernel, got_second)
        sums, small, parts[1], center = lax.optimization_barrier((sums, small, parts[1], center))
        held = [small, swap(small, "member", 8)]
        far = [across(sums, i) for i in range(1, planes)]
        far, held[1], parts = lax.optimization_barrier((far, held[1], parts))
        held.append(swap(jnp.concatenate(held, axis=0), "member", 4))
        gain, spread, mixed_second = solve([sums] + far, center)
        mixed_second, parts, held[2] = lax.optimization_barrier((mixed_second, parts, held[2]))
        new_second = exchange(mixed_second)

        held.append(swap(jnp.concatenate(held, axis=0), "member", 2))
        got_first = by_plane(parts).reshape(slabs_first.shape)
        mixed_first = blocked(mix_kernel, got_first, spread)
        mixed_first = mixed_first.reshape((planes, PLANE) + mixed_first.shape[1:])
        back, held[3] = lax.optimization_barrier((within(mixed_first), held[3]))
        held.append(swap(jnp.concatenate(held, axis=0), "member", 1))
        homes = [pick(back, plane ^ i, 1) for i in range(planes)]
        homes = [homes[0]] + [across(homes[i], i) for i in range(1, planes)]

        order = me[None]
        for bit in (8, 4, 2, 1):
            order = jnp.concatenate([order, order ^ bit])
        column = reorder(pick(gain, me, 1)[None], order)[0].astype(jnp.float32)
        new_small = mix_one(column, held)
        new_third = new_small[:outs].T
        new_bfirst = new_small[outs : outs + 1]
        new_bsecond = new_small[outs + 1 : outs + 2]
        new_second = blocked(copy_kernel, new_second)
        homes, new_second, new_third, new_bfirst, new_bsecond = lax.optimization_barrier(
            (homes, new_second, new_third, new_bfirst, new_bsecond)
        )
        new_first = place_parts(plane, homes)
    else:
        both = exchange(both)
        allpred, allres = both[:, 0], both[:, 1]
        devpred = allpred - jnp.mean(allpred, axis=0, keepdims=True)
        scaled = devpred / var_part
        sums = jnp.dot(
            scaled, jnp.concatenate([devpred, allres], axis=0).T, precision=lax.Precision.HIGHEST
        )
        sums = lax.psum(sums, ("member", "pair"))
        gain = solve_gain(sums[:, :members], sums[:, members:])
        gain_tr = gain.astype(jnp.bfloat16).T
        new_second = exchange(mix_plain(got_second, gain_tr))
        new_first = exchange(mix_plain(exchange(slabs_first), gain_tr))
        small = jnp.concatenate([third_w.T, b_first, b_second], axis=0)
        full = lax.all_gather(small, "member", axis=0)
        new_small = mix_plain(full, lax.dynamic_index_in_dim(gain_tr, me, 0))[0]
        new_third = new_small[:outs].T
        new_bfirst = new_small[outs : outs + 1]
        new_bsecond = new_small[outs + 1 :]
    return (
        new_first.reshape(w_first.shape),
        new_bfirst,
        new_second.reshape(w_second.shape),
        new_bsecond,
        new_third[None],
    )


def solution(mesh):
    in_specs = (
        P(),
        P("member", None, "pair"),
        P("member", "pair"),
        P("member", None, "pair"),
        P("member", "pair"),
        P("member", "pair", None),
        P(),
        P("member", None, None),
        P(),
    )
    out_specs = (
        P("member", None, "pair"),
        P("member", "pair"),
        P("member", None, "pair"),
        P("member", "pair"),
        P("member", "pair", None),
    )
    return jax.shard_map(body, mesh=mesh, in_specs=in_specs, out_specs=out_specs, check_vma=False)
```

```python
import functools

import jax
import jax.numpy as jnp
from jax import lax
from jax.experimental import pallas as pl
from jax.experimental.pallas import tpu as pltpu
from jax.sharding import PartitionSpec as P

ROW_BITS = 4
ROWS = 1 << ROW_BITS
PLANE = 4
TILE = 256
LOADS = 4
VMEM = 56 << 20
LIGHT = pl.CostEstimate(flops=1, bytes_accessed=1, transcendentals=0)


def solve_gain(amat, bmat):
    count = amat.shape[0]
    system = amat + count * jnp.eye(count, dtype=jnp.float32)
    factor = jnp.linalg.cholesky(system)
    middle = lax.linalg.triangular_solve(
        factor, bmat, left_side=True, lower=True, transpose_a=False
    )
    return lax.linalg.triangular_solve(factor, middle, left_side=True, lower=True, transpose_a=True)


def mix_rows(spread_ref, x_ref, y_ref, at):
    members, _, width = x_ref.shape
    for left in range(0, width, TILE):
        piece = (slice(None), pl.ds(at, ROWS), pl.ds(left, TILE))
        full = x_ref[piece].astype(jnp.float32)
        mean = jnp.sum(full, axis=0, keepdims=True) * (1.0 / members)
        center = (full - mean).astype(jnp.bfloat16).reshape(members * ROWS, TILE)
        mixed = jnp.dot(spread_ref[...], center, preferred_element_type=jnp.float32)
        y_ref[piece] = mixed.astype(jnp.bfloat16).reshape(members, ROWS, TILE)


def center_kernel(x_ref, y_ref):
    members, rows, width = x_ref.shape
    for at in range(0, rows, ROWS):
        for left in range(0, width, TILE):
            piece = (slice(None), pl.ds(at, ROWS), pl.ds(left, TILE))
            full = x_ref[piece].astype(jnp.float32)
            mean = jnp.sum(full, axis=0, keepdims=True) * (1.0 / members)
            y_ref[piece] = (full - mean).astype(jnp.bfloat16)


def apply_rows(spread_ref, x_ref, y_ref, at):
    members, _, width = x_ref.shape
    rows = (slice(None), pl.ds(at, ROWS), slice(None))
    center = x_ref[rows].reshape(members * ROWS, width)
    mixed = jnp.dot(spread_ref[...], center, preferred_element_type=jnp.float32)
    y_ref[rows] = mixed.astype(jnp.bfloat16).reshape(members, ROWS, width)


def mix_kernel(spread_ref, x_ref, y_ref):
    for at in range(0, x_ref.shape[1], ROWS):
        mix_rows(spread_ref, x_ref, y_ref, at)


def copy_kernel(x_ref, y_ref):
    y_ref[...] = x_ref[...]


def blocked(kernel, x, *wholes):
    members, total, width = x.shape
    rows = min(total, 4 * ROWS)
    block = pl.BlockSpec((members, rows, width), lambda i: (0, i, 0))
    return pl.pallas_call(
        kernel,
        grid=(total // rows,),
        in_specs=[pl.BlockSpec(w.shape, lambda i: (0, 0)) for w in wholes] + [block],
        out_specs=block,
        out_shape=jax.ShapeDtypeStruct(x.shape, jnp.bfloat16),
        compiler_params=pltpu.CompilerParams(vmem_limit_bytes=VMEM),
        cost_estimate=LIGHT,
    )(*wholes, x)


def moments_kernel(both_ref, var_ref, sums_ref):
    pred, resid = both_ref[:, 0, :], both_ref[:, 1, :]
    dev = pred - jnp.sum(pred, axis=0, keepdims=True) * (1.0 / pred.shape[0])
    scaled = dev / var_ref[...]
    sums_ref[...] = lax.dot_general(
        scaled,
        jnp.concatenate([dev, resid], axis=0),
        (((1,), (1,)), ((), ())),
        precision=lax.Precision.HIGHEST,
        preferred_element_type=jnp.float32,
    )


def whole_call(kernel, out_shape, *args):
    return pl.pallas_call(kernel, out_shape=out_shape, cost_estimate=LIGHT)(*args)


def solve_kernel(
    own_ref, far1_ref, far2_ref, far3_ref, x_ref, gain_ref, spread_ref, y_ref, x_buf, y_buf, x_sems, y_sems
):
    size = x_ref.shape[0] // LOADS
    loads = [
        pltpu.make_async_copy(
            x_ref.at[pl.ds(i * size, size)], x_buf.at[pl.ds(i * size, size)], x_sems.at[i]
        )
        for i in range(LOADS)
    ]
    for load in loads:
        load.start()
    total = (own_ref[...] + far1_ref[...]) + (far2_ref[...] + far3_ref[...])
    count = total.shape[0]
    row = lax.broadcasted_iota(jnp.int32, total.shape, 0)
    col = lax.broadcasted_iota(jnp.int32, total.shape, 1)
    total = total + jnp.where(row == col, float(count), 0.0)
    for k in range(count):
        pivot = total[k : k + 1, :] / total[k : k + 1, k : k + 1]
        total = jnp.where(row == k, pivot, total - total[:, k : k + 1] * pivot)
    gain = total[:, count:].astype(jnp.bfloat16)
    gain_ref[...] = gain
    size = count * ROWS
    row = lax.broadcasted_iota(jnp.int32, (size, count), 0)
    col = lax.broadcasted_iota(jnp.int32, (size, count), 1)
    expand = (row >> ROW_BITS == col).astype(jnp.bfloat16)
    wide = lax.dot_general(
        expand, gain, (((1,), (1,)), ((), ())), preferred_element_type=jnp.float32
    ).astype(jnp.bfloat16)
    wide = lax.dot_general(
        wide, expand, (((1,), (1,)), ((), ())), preferred_element_type=jnp.float32
    )
    at_row = lax.broadcasted_iota(jnp.int32, (size, size), 0)
    at_col = lax.broadcasted_iota(jnp.int32, (size, size), 1)
    same = ((at_row ^ at_col) & (ROWS - 1)) == 0
    spread_ref[...] = jnp.where(same, wide, 0.0).astype(jnp.bfloat16)

    for load in loads:
        load.wait()
    stores = []
    for i in range(x_ref.shape[1] // ROWS):
        rows = (slice(None), pl.ds(i * ROWS, ROWS), slice(None))
        apply_rows(spread_ref, x_buf, y_buf, i * ROWS)
        stores.append(pltpu.make_async_copy(y_buf.at[rows], y_ref.at[rows], y_sems.at[i]))
        stores[-1].start()
    for store in stores:
        store.wait()


def solve(sums, x):
    members = x.shape[0]
    size = members * ROWS
    vmem, anywhere = pl.BlockSpec(memory_space=pltpu.VMEM), pl.BlockSpec(memory_space=pl.ANY)
    return pl.pallas_call(
        solve_kernel,
        in_specs=[vmem] * len(sums) + [anywhere],
        out_specs=[vmem, vmem, anywhere],
        out_shape=[
            jax.ShapeDtypeStruct((members, members), jnp.bfloat16),
            jax.ShapeDtypeStruct((size, size), jnp.bfloat16),
            jax.ShapeDtypeStruct(x.shape, x.dtype),
        ],
        scratch_shapes=[
            pltpu.VMEM(x.shape, x.dtype),
            pltpu.VMEM(x.shape, x.dtype),
            pltpu.SemaphoreType.DMA((LOADS,)),
            pltpu.SemaphoreType.DMA((x.shape[1] // ROWS,)),
        ],
        compiler_params=pltpu.CompilerParams(vmem_limit_bytes=VMEM),
        cost_estimate=LIGHT,
    )(*sums, x)


def mix_plain(slab, gain_tr):
    full = slab.astype(jnp.float32)
    center = (full - jnp.mean(full, axis=0, keepdims=True)).astype(jnp.bfloat16)
    return jnp.einsum(
        "jk,krc->jrc", gain_tr, center, preferred_element_type=jnp.float32
    ).astype(jnp.bfloat16)


def mix_one(column, blocks):
    full = [block.astype(jnp.float32) for block in blocks]
    mean = sum(jnp.sum(block, axis=0) for block in full) * (1.0 / column.shape[0])
    total = jnp.zeros_like(mean)
    at = 0
    for block in full:
        count = block.shape[0]
        center = (block - mean).astype(jnp.bfloat16).astype(jnp.float32)
        total = total + jnp.sum(center * column[at : at + count, None, None], axis=0)
        at += count
    return total.astype(jnp.bfloat16)


def place_kernel(at_ref, *refs):
    parts, out_ref, sems = refs[:-2], refs[-2], refs[-1]
    size = parts[0].shape[0]
    copies = [
        pltpu.make_async_copy(
            part, out_ref.at[pl.ds((at_ref[0] ^ flip) * size, size)], sems.at[flip]
        )
        for flip, part in enumerate(parts)
    ]
    for copy in copies:
        copy.start()
    for copy in copies:
        copy.wait()


def place_parts(at, parts):
    count, shape = len(parts), parts[0].shape
    return pl.pallas_call(
        place_kernel,
        in_specs=[pl.BlockSpec(memory_space=pltpu.SMEM)]
        + [pl.BlockSpec(memory_space=pltpu.VMEM)] * count,
        out_specs=pl.BlockSpec(memory_space=pl.ANY),
        out_shape=jax.ShapeDtypeStruct((count * shape[0],) + shape[1:], parts[0].dtype),
        scratch_shapes=[pltpu.SemaphoreType.DMA((count,))],
        compiler_params=pltpu.CompilerParams(vmem_limit_bytes=32 << 20),
        cost_estimate=LIGHT,
    )(at[None], *parts)


def first_kernel(scale, x_ref, w_ref, b_ref, y_ref):
    summed = jnp.dot(x_ref[...], w_ref[...], preferred_element_type=jnp.float32)
    y = jax.nn.gelu(summed * scale + b_ref[...].astype(jnp.float32), approximate=True)
    y_ref[...] = y.astype(jnp.bfloat16)


def first_layer(x, w, b, part):
    rows, depth = x.shape
    half = w.shape[1] // 2
    step = min(TILE, half)
    first = part * (half // step)
    return pl.pallas_call(
        functools.partial(first_kernel, depth ** (-0.5)),
        grid=(half // step,),
        in_specs=[
            pl.BlockSpec((rows, depth), lambda i: (0, 0)),
            pl.BlockSpec((depth, step), lambda i: (0, i + first)),
            pl.BlockSpec((1, step), lambda i: (0, i + first)),
        ],
        out_specs=pl.BlockSpec((rows, step), lambda i: (0, i)),
        out_shape=jax.ShapeDtypeStruct((rows, half), jnp.bfloat16),
        compiler_params=pltpu.CompilerParams(vmem_limit_bytes=32 << 20),
        cost_estimate=LIGHT,
    )(x, w, b)


def second_kernel(scale, side_ref, *refs):
    inputs, weights, (b_ref, third_ref, y_ref) = refs[:4], refs[4:8], refs[8:]
    summed = sum(
        jnp.dot(x_ref[...], w_ref[...], preferred_element_type=jnp.float32)
        for x_ref, w_ref in zip(inputs, weights)
    )
    y = jax.nn.gelu(summed * scale + b_ref[...].astype(jnp.float32), approximate=True)
    part = lax.dot_general(
        third_ref[...],
        y.astype(jnp.bfloat16),
        (((1,), (1,)), ((), ())),
        preferred_element_type=jnp.float32,
    )

    @pl.when(pl.program_id(0) == 0)
    def _():
        y_ref[...] = jnp.zeros_like(y_ref)

    y_ref[...] += part * scale


def second_and_third(side, mine, other, w, b, third):
    rows, depth = mine[0].shape
    outs = third.shape[0]
    step = min(TILE, w.shape[1])
    whole = pl.BlockSpec((rows, depth), lambda i, side: (0, 0))
    return pl.pallas_call(
        functools.partial(second_kernel, w.shape[0] ** (-0.5)),
        grid_spec=pltpu.PrefetchScalarGridSpec(
            num_scalar_prefetch=1,
            grid=(w.shape[1] // step,),
            in_specs=[whole] * 4
            + [
                pl.BlockSpec((depth, step), lambda i, side: (2 * side[0], i)),
                pl.BlockSpec((depth, step), lambda i, side: (2 * side[0] + 1, i)),
                pl.BlockSpec((depth, step), lambda i, side: (2 - 2 * side[0], i)),
                pl.BlockSpec((depth, step), lambda i, side: (3 - 2 * side[0], i)),
                pl.BlockSpec((1, step), lambda i, side: (0, i)),
                pl.BlockSpec((outs, step), lambda i, side: (0, i)),
            ],
            out_specs=pl.BlockSpec((outs, rows), lambda i, side: (0, 0)),
        ),
        out_shape=jax.ShapeDtypeStruct((outs, rows), jnp.float32),
        compiler_params=pltpu.CompilerParams(vmem_limit_bytes=32 << 20),
        cost_estimate=LIGHT,
    )(side[None], *mine, *other, w, w, w, w, b, third)


def exchange(x):
    return lax.all_to_all(x, "member", split_axis=0, concat_axis=0, tiled=True)


def swap(x, axis, bit):
    count = lax.axis_size(axis)
    return lax.ppermute(x, axis, [(i, i ^ bit) for i in range(count)])


def reorder(gain_tr, order):
    pick = (order[None, :] == jnp.arange(gain_tr.shape[1])[:, None]).astype(jnp.bfloat16)
    return jnp.dot(gain_tr, pick, preferred_element_type=jnp.float32).astype(jnp.bfloat16)


def pick(x, at, axis=0):
    return lax.dynamic_index_in_dim(x, at, axis, keepdims=False)


def after(value, earlier):
    return lax.optimization_barrier((value, earlier))[0]


def body(samples, w_first, b_first, w_second, b_second, w_third, observed, perturb, variance):
    members = lax.axis_size("member")
    me = lax.axis_index("member")
    side = lax.axis_index("pair")
    width = w_first.shape[2]
    first_w, second_w, third_w = w_first[0], w_second[0], w_third[0]
    slabs_first = first_w.reshape(members, -1, width)
    slabs_second = second_w.reshape(members, -1, width)
    outs = third_w.shape[1]
    fast = members == PLANE * PLANE and width % TILE == 0
    planes = members // PLANE
    plane, place = me // PLANE, me % PLANE

    def across(x, flip):
        return swap(x, "member", flip * PLANE)

    first = [first_layer(samples, first_w, b_first, i) for i in range(2)]
    other = [swap(x, "pair", 1) for x in first]
    partial_out = second_and_third(side, first, other, second_w, b_second, third_w.T)

    half = partial_out.shape[1] // 2
    start = side * half
    keep = lax.dynamic_slice_in_dim(partial_out, start, half, 1)
    give = lax.dynamic_slice_in_dim(partial_out, (1 - side) * half, half, 1)
    pred = keep + swap(give, "pair", 1)
    observed_half = lax.dynamic_slice_in_dim(observed.T, start, half, 1)
    variance_half = lax.dynamic_slice_in_dim(variance.T, start, half, 1)
    perturb_half = lax.dynamic_slice_in_dim(perturb[0].T, start, half, 1)
    resid = observed_half + jnp.sqrt(variance_half) * perturb_half - pred
    count = pred.size // members
    both = jnp.concatenate(
        [pred.reshape(members, 1, count), resid.reshape(members, 1, count)], axis=1
    )
    got_second = exchange(slabs_second)
    var_part = lax.dynamic_index_in_dim(variance_half.reshape(members, count), me, 0)
    if fast:
        def by_plane(parts):
            parts = jnp.stack(parts)
            return jnp.stack([pick(parts, plane ^ i) for i in range(planes)])

        def within(x):
            parts = [pick(x, place ^ i, 1) for i in range(PLANE)]
            parts = jnp.stack([parts[0]] + [swap(parts[i], "member", i) for i in range(1, PLANE)])
            return jnp.stack([pick(parts, place ^ i) for i in range(PLANE)])

        slabs = within(slabs_first.reshape((planes, PLANE) + slabs_first.shape[1:]))
        both, slabs = lax.optimization_barrier((both, slabs))
        both = within(both.reshape((planes, PLANE) + both.shape[1:]))
        parts = [pick(both, plane ^ i, 1) for i in range(planes)]
        parts = [parts[0]] + [across(parts[i], i) for i in range(1, planes)]
        small = jnp.concatenate([third_w.T, b_first, b_second], axis=0)
        slabs = [pick(slabs, plane ^ i, 1) for i in range(planes)]
        joined = jnp.concatenate([slabs[2].reshape(-1, width), small], axis=0)
        parts, slabs, joined = lax.optimization_barrier((parts, slabs, joined))
        both = jnp.concatenate(by_plane(parts), axis=0)
        joined = across(joined, 2)
        size = joined.shape[0] - small.shape[0]
        held = [small[None], joined[None, size:]]
        parts = [
            slabs[0],
            across(slabs[1], 1),
            joined[:size].reshape(slabs[2].shape),
            across(slabs[3], 3),
        ]
        sums = whole_call(
            moments_kernel,
            jax.ShapeDtypeStruct((members, 2 * members), jnp.float32),
            both,
            var_part,
        )
        sums = sums + swap(sums, "pair", 1)
        sums = sums + swap(sums, "member", 1)
        sums = sums + swap(sums, "member", 2)
        center = blocked(center_kernel, got_second)
        sums, parts[1], parts[3], center = lax.optimization_barrier((sums, parts[1], parts[3], center))
        far = [across(sums, i) for i in range(1, planes)]
        far, held[1], parts = lax.optimization_barrier((far, held[1], parts))
        held.append(swap(jnp.concatenate(held, axis=0), "member", 4))
        gain, spread, mixed_second = solve([sums] + far, center)
        mixed_second, parts, held[2] = lax.optimization_barrier((mixed_second, parts, held[2]))
        new_second = exchange(mixed_second)

        held.append(swap(jnp.concatenate(held, axis=0), "member", 2))
        got_first = by_plane(parts).reshape(slabs_first.shape)
        mixed_first = blocked(mix_kernel, got_first, spread)
        mixed_first = mixed_first.reshape((planes, PLANE) + mixed_first.shape[1:])
        back, held[3] = lax.optimization_barrier((within(mixed_first), held[3]))
        held.append(swap(jnp.concatenate(held, axis=0), "member", 1))
        homes = [pick(back, plane ^ i, 1) for i in range(planes)]
        homes = [homes[0]] + [across(homes[i], i) for i in range(1, planes)]

        order = me[None]
        for bit in (8, 4, 2, 1):
            order = jnp.concatenate([order, order ^ bit])
        column = reorder(pick(gain, me, 1)[None], order)[0].astype(jnp.float32)
        new_small = mix_one(column, held)
        new_third = new_small[:outs].T
        new_bfirst = new_small[outs : outs + 1]
        new_bsecond = new_small[outs + 1 : outs + 2]
        new_second = blocked(copy_kernel, new_second)
        homes, new_second, new_third, new_bfirst, new_bsecond = lax.optimization_barrier(
            (homes, new_second, new_third, new_bfirst, new_bsecond)
        )
        new_first = place_parts(plane, homes)
    else:
        both = exchange(both)
        allpred, allres = both[:, 0], both[:, 1]
        devpred = allpred - jnp.mean(allpred, axis=0, keepdims=True)
        scaled = devpred / var_part
        sums = jnp.dot(
            scaled, jnp.concatenate([devpred, allres], axis=0).T, precision=lax.Precision.HIGHEST
        )
        sums = lax.psum(sums, ("member", "pair"))
        gain = solve_gain(sums[:, :members], sums[:, members:])
        gain_tr = gain.astype(jnp.bfloat16).T
        new_second = exchange(mix_plain(got_second, gain_tr))
        new_first = exchange(mix_plain(exchange(slabs_first), gain_tr))
        small = jnp.concatenate([third_w.T, b_first, b_second], axis=0)
        full = lax.all_gather(small, "member", axis=0)
        new_small = mix_plain(full, lax.dynamic_index_in_dim(gain_tr, me, 0))[0]
        new_third = new_small[:outs].T
        new_bfirst = new_small[outs : outs + 1]
        new_bsecond = new_small[outs + 1 :]
    return (
        new_first.reshape(w_first.shape),
        new_bfirst,
        new_second.reshape(w_second.shape),
        new_bsecond,
        new_third[None],
    )


def solution(mesh):
    in_specs = (
        P(),
        P("member", None, "pair"),
        P("member", "pair"),
        P("member", None, "pair"),
        P("member", "pair"),
        P("member", "pair", None),
        P(),
        P("member", None, None),
        P(),
    )
    out_specs = (
        P("member", None, "pair"),
        P("member", "pair"),
        P("member", None, "pair"),
        P("member", "pair"),
        P("member", "pair", None),
    )
    return jax.shard_map(body, mesh=mesh, in_specs=in_specs, out_specs=out_specs, check_vma=False)
```

```python
import functools

import jax
import jax.numpy as jnp
from jax import lax
from jax.experimental import pallas as pl
from jax.experimental.pallas import tpu as pltpu
from jax.sharding import PartitionSpec as P

ROW_BITS = 4
ROWS = 1 << ROW_BITS
PLANE = 4
TILE = 256
LOADS = 4
VMEM = 56 << 20
LIGHT = pl.CostEstimate(flops=1, bytes_accessed=1, transcendentals=0)


def solve_gain(amat, bmat):
    count = amat.shape[0]
    system = amat + count * jnp.eye(count, dtype=jnp.float32)
    factor = jnp.linalg.cholesky(system)
    middle = lax.linalg.triangular_solve(
        factor, bmat, left_side=True, lower=True, transpose_a=False
    )
    return lax.linalg.triangular_solve(factor, middle, left_side=True, lower=True, transpose_a=True)


def mix_rows(spread_ref, x_ref, y_ref, at):
    members, _, width = x_ref.shape
    for left in range(0, width, TILE):
        piece = (slice(None), pl.ds(at, ROWS), pl.ds(left, TILE))
        full = x_ref[piece].astype(jnp.float32)
        mean = jnp.sum(full, axis=0, keepdims=True) * (1.0 / members)
        center = (full - mean).astype(jnp.bfloat16).reshape(members * ROWS, TILE)
        mixed = jnp.dot(spread_ref[...], center, preferred_element_type=jnp.float32)
        y_ref[piece] = mixed.astype(jnp.bfloat16).reshape(members, ROWS, TILE)


def center_kernel(x_ref, y_ref):
    members, rows, width = x_ref.shape
    for at in range(0, rows, ROWS):
        for left in range(0, width, TILE):
            piece = (slice(None), pl.ds(at, ROWS), pl.ds(left, TILE))
            full = x_ref[piece].astype(jnp.float32)
            mean = jnp.sum(full, axis=0, keepdims=True) * (1.0 / members)
            y_ref[piece] = (full - mean).astype(jnp.bfloat16)


def apply_rows(spread_ref, x_ref, y_ref, at):
    members, _, width = x_ref.shape
    rows = (slice(None), pl.ds(at, ROWS), slice(None))
    center = x_ref[rows].reshape(members * ROWS, width)
    mixed = jnp.dot(spread_ref[...], center, preferred_element_type=jnp.float32)
    y_ref[rows] = mixed.astype(jnp.bfloat16).reshape(members, ROWS, width)


def mix_kernel(spread_ref, x_ref, y_ref):
    for at in range(0, x_ref.shape[1], ROWS):
        mix_rows(spread_ref, x_ref, y_ref, at)


def copy_kernel(x_ref, y_ref):
    y_ref[...] = x_ref[...]


def blocked(kernel, x, *wholes):
    members, total, width = x.shape
    rows = min(total, 4 * ROWS)
    block = pl.BlockSpec((members, rows, width), lambda i: (0, i, 0))
    return pl.pallas_call(
        kernel,
        grid=(total // rows,),
        in_specs=[pl.BlockSpec(w.shape, lambda i: (0, 0)) for w in wholes] + [block],
        out_specs=block,
        out_shape=jax.ShapeDtypeStruct(x.shape, jnp.bfloat16),
        compiler_params=pltpu.CompilerParams(vmem_limit_bytes=VMEM),
        cost_estimate=LIGHT,
    )(*wholes, x)


def moments_kernel(both_ref, var_ref, sums_ref):
    pred, resid = both_ref[:, 0, :], both_ref[:, 1, :]
    dev = pred - jnp.sum(pred, axis=0, keepdims=True) * (1.0 / pred.shape[0])
    scaled = dev / var_ref[...]
    sums_ref[...] = lax.dot_general(
        scaled,
        jnp.concatenate([dev, resid], axis=0),
        (((1,), (1,)), ((), ())),
        precision=lax.Precision.HIGHEST,
        preferred_element_type=jnp.float32,
    )


def whole_call(kernel, out_shape, *args):
    return pl.pallas_call(kernel, out_shape=out_shape, cost_estimate=LIGHT)(*args)


def solve_kernel(
    own_ref, far1_ref, far2_ref, far3_ref, x_ref, gain_ref, spread_ref, y_ref, x_buf, y_buf, x_sems, y_sems
):
    size = x_ref.shape[0] // LOADS
    loads = [
        pltpu.make_async_copy(
            x_ref.at[pl.ds(i * size, size)], x_buf.at[pl.ds(i * size, size)], x_sems.at[i]
        )
        for i in range(LOADS)
    ]
    for load in loads:
        load.start()
    total = (own_ref[...] + far1_ref[...]) + (far2_ref[...] + far3_ref[...])
    count = total.shape[0]
    row = lax.broadcasted_iota(jnp.int32, total.shape, 0)
    col = lax.broadcasted_iota(jnp.int32, total.shape, 1)
    total = total + jnp.where(row == col, float(count), 0.0)
    for k in range(count):
        pivot = total[k : k + 1, :] / total[k : k + 1, k : k + 1]
        total = jnp.where(row == k, pivot, total - total[:, k : k + 1] * pivot)
    gain = total[:, count:].astype(jnp.bfloat16)
    gain_ref[...] = gain
    size = count * ROWS
    row = lax.broadcasted_iota(jnp.int32, (size, count), 0)
    col = lax.broadcasted_iota(jnp.int32, (size, count), 1)
    expand = (row >> ROW_BITS == col).astype(jnp.bfloat16)
    wide = lax.dot_general(
        expand, gain, (((1,), (1,)), ((), ())), preferred_element_type=jnp.float32
    ).astype(jnp.bfloat16)
    wide = lax.dot_general(
        wide, expand, (((1,), (1,)), ((), ())), preferred_element_type=jnp.float32
    )
    at_row = lax.broadcasted_iota(jnp.int32, (size, size), 0)
    at_col = lax.broadcasted_iota(jnp.int32, (size, size), 1)
    same = ((at_row ^ at_col) & (ROWS - 1)) == 0
    spread_ref[...] = jnp.where(same, wide, 0.0).astype(jnp.bfloat16)

    for load in loads:
        load.wait()
    stores = []
    for i in range(x_ref.shape[1] // ROWS):
        rows = (slice(None), pl.ds(i * ROWS, ROWS), slice(None))
        apply_rows(spread_ref, x_buf, y_buf, i * ROWS)
        stores.append(pltpu.make_async_copy(y_buf.at[rows], y_ref.at[rows], y_sems.at[i]))
        stores[-1].start()
    for store in stores:
        store.wait()


def solve(sums, x):
    members = x.shape[0]
    size = members * ROWS
    vmem, anywhere = pl.BlockSpec(memory_space=pltpu.VMEM), pl.BlockSpec(memory_space=pl.ANY)
    return pl.pallas_call(
        solve_kernel,
        in_specs=[vmem] * len(sums) + [anywhere],
        out_specs=[vmem, vmem, anywhere],
        out_shape=[
            jax.ShapeDtypeStruct((members, members), jnp.bfloat16),
            jax.ShapeDtypeStruct((size, size), jnp.bfloat16),
            jax.ShapeDtypeStruct(x.shape, x.dtype),
        ],
        scratch_shapes=[
            pltpu.VMEM(x.shape, x.dtype),
            pltpu.VMEM(x.shape, x.dtype),
            pltpu.SemaphoreType.DMA((LOADS,)),
            pltpu.SemaphoreType.DMA((x.shape[1] // ROWS,)),
        ],
        compiler_params=pltpu.CompilerParams(vmem_limit_bytes=VMEM),
        cost_estimate=LIGHT,
    )(*sums, x)


def mix_plain(slab, gain_tr):
    full = slab.astype(jnp.float32)
    center = (full - jnp.mean(full, axis=0, keepdims=True)).astype(jnp.bfloat16)
    return jnp.einsum(
        "jk,krc->jrc", gain_tr, center, preferred_element_type=jnp.float32
    ).astype(jnp.bfloat16)


def mix_one(column, blocks):
    full = [block.astype(jnp.float32) for block in blocks]
    mean = sum(jnp.sum(block, axis=0) for block in full) * (1.0 / column.shape[0])
    total = jnp.zeros_like(mean)
    at = 0
    for block in full:
        count = block.shape[0]
        center = (block - mean).astype(jnp.bfloat16).astype(jnp.float32)
        total = total + jnp.sum(center * column[at : at + count, None, None], axis=0)
        at += count
    return total.astype(jnp.bfloat16)


def place_kernel(at_ref, *refs):
    parts, out_ref, sems = refs[:-2], refs[-2], refs[-1]
    size = parts[0].shape[0]
    copies = [
        pltpu.make_async_copy(
            part, out_ref.at[pl.ds((at_ref[0] ^ flip) * size, size)], sems.at[flip]
        )
        for flip, part in enumerate(parts)
    ]
    for copy in copies:
        copy.start()
    for copy in copies:
        copy.wait()


def place_parts(at, parts):
    count, shape = len(parts), parts[0].shape
    return pl.pallas_call(
        place_kernel,
        in_specs=[pl.BlockSpec(memory_space=pltpu.SMEM)]
        + [pl.BlockSpec(memory_space=pltpu.VMEM)] * count,
        out_specs=pl.BlockSpec(memory_space=pl.ANY),
        out_shape=jax.ShapeDtypeStruct((count * shape[0],) + shape[1:], parts[0].dtype),
        scratch_shapes=[pltpu.SemaphoreType.DMA((count,))],
        compiler_params=pltpu.CompilerParams(vmem_limit_bytes=32 << 20),
        cost_estimate=LIGHT,
    )(at[None], *parts)


def first_kernel(scale, x_ref, w_ref, b_ref, y_ref):
    summed = jnp.dot(x_ref[...], w_ref[...], preferred_element_type=jnp.float32)
    y = jax.nn.gelu(summed * scale + b_ref[...].astype(jnp.float32), approximate=True)
    y_ref[...] = y.astype(jnp.bfloat16)


def first_layer(x, w, b, part):
    rows, depth = x.shape
    half = w.shape[1] // 2
    step = min(TILE, half)
    first = part * (half // step)
    return pl.pallas_call(
        functools.partial(first_kernel, depth ** (-0.5)),
        grid=(half // step,),
        in_specs=[
            pl.BlockSpec((rows, depth), lambda i: (0, 0)),
            pl.BlockSpec((depth, step), lambda i: (0, i + first)),
            pl.BlockSpec((1, step), lambda i: (0, i + first)),
        ],
        out_specs=pl.BlockSpec((rows, step), lambda i: (0, i)),
        out_shape=jax.ShapeDtypeStruct((rows, half), jnp.bfloat16),
        compiler_params=pltpu.CompilerParams(vmem_limit_bytes=32 << 20),
        cost_estimate=LIGHT,
    )(x, w, b)


def second_kernel(scale, side_ref, *refs):
    inputs, weights, (b_ref, third_ref, y_ref) = refs[:4], refs[4:8], refs[8:]
    summed = sum(
        jnp.dot(x_ref[...], w_ref[...], preferred_element_type=jnp.float32)
        for x_ref, w_ref in zip(inputs, weights)
    )
    y = jax.nn.gelu(summed * scale + b_ref[...].astype(jnp.float32), approximate=True)
    part = lax.dot_general(
        third_ref[...],
        y.astype(jnp.bfloat16),
        (((1,), (1,)), ((), ())),
        preferred_element_type=jnp.float32,
    )

    @pl.when(pl.program_id(0) == 0)
    def _():
        y_ref[...] = jnp.zeros_like(y_ref)

    y_ref[...] += part * scale


def second_and_third(side, mine, other, w, b, third):
    rows, depth = mine[0].shape
    outs = third.shape[0]
    step = min(TILE, w.shape[1])
    whole = pl.BlockSpec((rows, depth), lambda i, side: (0, 0))
    return pl.pallas_call(
        functools.partial(second_kernel, w.shape[0] ** (-0.5)),
        grid_spec=pltpu.PrefetchScalarGridSpec(
            num_scalar_prefetch=1,
            grid=(w.shape[1] // step,),
            in_specs=[whole] * 4
            + [
                pl.BlockSpec((depth, step), lambda i, side: (2 * side[0], i)),
                pl.BlockSpec((depth, step), lambda i, side: (2 * side[0] + 1, i)),
                pl.BlockSpec((depth, step), lambda i, side: (2 - 2 * side[0], i)),
                pl.BlockSpec((depth, step), lambda i, side: (3 - 2 * side[0], i)),
                pl.BlockSpec((1, step), lambda i, side: (0, i)),
                pl.BlockSpec((outs, step), lambda i, side: (0, i)),
            ],
            out_specs=pl.BlockSpec((outs, rows), lambda i, side: (0, 0)),
        ),
        out_shape=jax.ShapeDtypeStruct((outs, rows), jnp.float32),
        compiler_params=pltpu.CompilerParams(vmem_limit_bytes=32 << 20),
        cost_estimate=LIGHT,
    )(side[None], *mine, *other, w, w, w, w, b, third)


def exchange(x):
    return lax.all_to_all(x, "member", split_axis=0, concat_axis=0, tiled=True)


def swap(x, axis, bit):
    count = lax.axis_size(axis)
    return lax.ppermute(x, axis, [(i, i ^ bit) for i in range(count)])


def reorder(gain_tr, order):
    pick = (order[None, :] == jnp.arange(gain_tr.shape[1])[:, None]).astype(jnp.bfloat16)
    return jnp.dot(gain_tr, pick, preferred_element_type=jnp.float32).astype(jnp.bfloat16)


def pick(x, at, axis=0):
    return lax.dynamic_index_in_dim(x, at, axis, keepdims=False)


def after(value, earlier):
    return lax.optimization_barrier((value, earlier))[0]


def body(samples, w_first, b_first, w_second, b_second, w_third, observed, perturb, variance):
    members = lax.axis_size("member")
    me = lax.axis_index("member")
    side = lax.axis_index("pair")
    width = w_first.shape[2]
    first_w, second_w, third_w = w_first[0], w_second[0], w_third[0]
    slabs_first = first_w.reshape(members, -1, width)
    slabs_second = second_w.reshape(members, -1, width)
    outs = third_w.shape[1]
    fast = members == PLANE * PLANE and width % TILE == 0
    planes = members // PLANE
    plane, place = me // PLANE, me % PLANE

    def across(x, flip):
        return swap(x, "member", flip * PLANE)

    first = [first_layer(samples, first_w, b_first, i) for i in range(2)]
    other = [swap(x, "pair", 1) for x in first]
    partial_out = second_and_third(side, first, other, second_w, b_second, third_w.T)

    half = partial_out.shape[1] // 2
    start = side * half
    keep = lax.dynamic_slice_in_dim(partial_out, start, half, 1)
    give = lax.dynamic_slice_in_dim(partial_out, (1 - side) * half, half, 1)
    pred = keep + swap(give, "pair", 1)
    observed_half = lax.dynamic_slice_in_dim(observed.T, start, half, 1)
    variance_half = lax.dynamic_slice_in_dim(variance.T, start, half, 1)
    perturb_half = lax.dynamic_slice_in_dim(perturb[0].T, start, half, 1)
    resid = observed_half + jnp.sqrt(variance_half) * perturb_half - pred
    count = pred.size // members
    both = jnp.concatenate(
        [pred.reshape(members, 1, count), resid.reshape(members, 1, count)], axis=1
    )
    got_second = exchange(slabs_second)
    var_part = lax.dynamic_index_in_dim(variance_half.reshape(members, count), me, 0)
    if fast:
        def by_plane(parts):
            parts = jnp.stack(parts)
            return jnp.stack([pick(parts, plane ^ i) for i in range(planes)])

        def within(x):
            parts = [pick(x, place ^ i, 1) for i in range(PLANE)]
            parts = jnp.stack([parts[0]] + [swap(parts[i], "member", i) for i in range(1, PLANE)])
            return jnp.stack([pick(parts, place ^ i) for i in range(PLANE)])

        slabs = after(slabs_first, partial_out)
        slabs = within(slabs.reshape((planes, PLANE) + slabs.shape[1:]))
        both = within(both.reshape((planes, PLANE) + both.shape[1:]))
        parts = [pick(both, plane ^ i, 1) for i in range(planes)]
        parts = [parts[0]] + [across(parts[i], i) for i in range(1, planes)]
        small = jnp.concatenate([third_w.T, b_first, b_second], axis=0)
        slabs = [pick(slabs, plane ^ i, 1) for i in range(planes)]
        joined = jnp.concatenate([slabs[2].reshape(-1, width), small], axis=0)
        parts, slabs, joined = lax.optimization_barrier((parts, slabs, joined))
        both = jnp.concatenate(by_plane(parts), axis=0)
        joined = across(joined, 2)
        size = joined.shape[0] - small.shape[0]
        held = [small[None], joined[None, size:]]
        parts = [
            slabs[0],
            across(slabs[1], 1),
            joined[:size].reshape(slabs[2].shape),
            across(slabs[3], 3),
        ]
        sums = whole_call(
            moments_kernel,
            jax.ShapeDtypeStruct((members, 2 * members), jnp.float32),
            both,
            var_part,
        )
        sums = sums + swap(sums, "pair", 1)
        sums = sums + swap(sums, "member", 1)
        sums = sums + swap(sums, "member", 2)
        center = blocked(center_kernel, got_second)
        sums, parts[1], parts[3], center = lax.optimization_barrier((sums, parts[1], parts[3], center))
        far = [across(sums, i) for i in range(1, planes)]
        far, held[1], parts = lax.optimization_barrier((far, held[1], parts))
        held.append(swap(jnp.concatenate(held, axis=0), "member", 4))
        gain, spread, mixed_second = solve([sums] + far, center)
        mixed_second, parts, held[2] = lax.optimization_barrier((mixed_second, parts, held[2]))
        new_second = exchange(mixed_second)

        held.append(swap(jnp.concatenate(held, axis=0), "member", 2))
        got_first = by_plane(parts).reshape(slabs_first.shape)
        mixed_first = blocked(mix_kernel, got_first, spread)
        mixed_first = mixed_first.reshape((planes, PLANE) + mixed_first.shape[1:])
        back, held[3] = lax.optimization_barrier((within(mixed_first), held[3]))
        held.append(swap(jnp.concatenate(held, axis=0), "member", 1))
        homes = [pick(back, plane ^ i, 1) for i in range(planes)]
        homes = [homes[0]] + [across(homes[i], i) for i in range(1, planes)]

        order = me[None]
        for bit in (8, 4, 2, 1):
            order = jnp.concatenate([order, order ^ bit])
        column = reorder(pick(gain, me, 1)[None], order)[0].astype(jnp.float32)
        new_small = mix_one(column, held)
        new_third = new_small[:outs].T
        new_bfirst = new_small[outs : outs + 1]
        new_bsecond = new_small[outs + 1 : outs + 2]
        new_second = blocked(copy_kernel, new_second)
        homes, new_second, new_third, new_bfirst, new_bsecond = lax.optimization_barrier(
            (homes, new_second, new_third, new_bfirst, new_bsecond)
        )
        new_first = place_parts(plane, homes)
    else:
        both = exchange(both)
        allpred, allres = both[:, 0], both[:, 1]
        devpred = allpred - jnp.mean(allpred, axis=0, keepdims=True)
        scaled = devpred / var_part
        sums = jnp.dot(
            scaled, jnp.concatenate([devpred, allres], axis=0).T, precision=lax.Precision.HIGHEST
        )
        sums = lax.psum(sums, ("member", "pair"))
        gain = solve_gain(sums[:, :members], sums[:, members:])
        gain_tr = gain.astype(jnp.bfloat16).T
        new_second = exchange(mix_plain(got_second, gain_tr))
        new_first = exchange(mix_plain(exchange(slabs_first), gain_tr))
        small = jnp.concatenate([third_w.T, b_first, b_second], axis=0)
        full = lax.all_gather(small, "member", axis=0)
        new_small = mix_plain(full, lax.dynamic_index_in_dim(gain_tr, me, 0))[0]
        new_third = new_small[:outs].T
        new_bfirst = new_small[outs : outs + 1]
        new_bsecond = new_small[outs + 1 :]
    return (
        new_first.reshape(w_first.shape),
        new_bfirst,
        new_second.reshape(w_second.shape),
        new_bsecond,
        new_third[None],
    )


def solution(mesh):
    in_specs = (
        P(),
        P("member", None, "pair"),
        P("member", "pair"),
        P("member", None, "pair"),
        P("member", "pair"),
        P("member", "pair", None),
        P(),
        P("member", None, None),
        P(),
    )
    out_specs = (
        P("member", None, "pair"),
        P("member", "pair"),
        P("member", None, "pair"),
        P("member", "pair"),
        P("member", "pair", None),
    )
    return jax.shard_map(body, mesh=mesh, in_specs=in_specs, out_specs=out_specs, check_vma=False)
```

```python
import functools

import jax
import jax.numpy as jnp
from jax import lax
from jax.experimental import pallas as pl
from jax.experimental.pallas import tpu as pltpu
from jax.sharding import PartitionSpec as P

ROW_BITS = 4
ROWS = 1 << ROW_BITS
PLANE = 4
TILE = 256
LOADS = 4
VMEM = 56 << 20
LIGHT = pl.CostEstimate(flops=1, bytes_accessed=1, transcendentals=0)


def solve_gain(amat, bmat):
    count = amat.shape[0]
    system = amat + count * jnp.eye(count, dtype=jnp.float32)
    factor = jnp.linalg.cholesky(system)
    middle = lax.linalg.triangular_solve(
        factor, bmat, left_side=True, lower=True, transpose_a=False
    )
    return lax.linalg.triangular_solve(factor, middle, left_side=True, lower=True, transpose_a=True)


def mix_rows(spread_ref, x_ref, y_ref, at):
    members, _, width = x_ref.shape
    for left in range(0, width, TILE):
        piece = (slice(None), pl.ds(at, ROWS), pl.ds(left, TILE))
        full = x_ref[piece].astype(jnp.float32)
        mean = jnp.sum(full, axis=0, keepdims=True) * (1.0 / members)
        center = (full - mean).astype(jnp.bfloat16).reshape(members * ROWS, TILE)
        mixed = jnp.dot(spread_ref[...], center, preferred_element_type=jnp.float32)
        y_ref[piece] = mixed.astype(jnp.bfloat16).reshape(members, ROWS, TILE)


def center_kernel(x_ref, y_ref):
    members, rows, width = x_ref.shape
    for at in range(0, rows, ROWS):
        for left in range(0, width, TILE):
            piece = (slice(None), pl.ds(at, ROWS), pl.ds(left, TILE))
            full = x_ref[piece].astype(jnp.float32)
            mean = jnp.sum(full, axis=0, keepdims=True) * (1.0 / members)
            y_ref[piece] = (full - mean).astype(jnp.bfloat16)


def apply_rows(spread_ref, x_ref, y_ref, at):
    members, _, width = x_ref.shape
    rows = (slice(None), pl.ds(at, ROWS), slice(None))
    center = x_ref[rows].reshape(members * ROWS, width)
    mixed = jnp.dot(spread_ref[...], center, preferred_element_type=jnp.float32)
    y_ref[rows] = mixed.astype(jnp.bfloat16).reshape(members, ROWS, width)


def mix_kernel(spread_ref, x_ref, y_ref):
    for at in range(0, x_ref.shape[1], ROWS):
        mix_rows(spread_ref, x_ref, y_ref, at)


def copy_kernel(x_ref, y_ref):
    y_ref[...] = x_ref[...]


def blocked(kernel, x, *wholes):
    members, total, width = x.shape
    rows = min(total, 4 * ROWS)
    block = pl.BlockSpec((members, rows, width), lambda i: (0, i, 0))
    return pl.pallas_call(
        kernel,
        grid=(total // rows,),
        in_specs=[pl.BlockSpec(w.shape, lambda i: (0, 0)) for w in wholes] + [block],
        out_specs=block,
        out_shape=jax.ShapeDtypeStruct(x.shape, jnp.bfloat16),
        compiler_params=pltpu.CompilerParams(vmem_limit_bytes=VMEM),
        cost_estimate=LIGHT,
    )(*wholes, x)


def moments_kernel(both_ref, var_ref, sums_ref):
    pred, resid = both_ref[:, 0, :], both_ref[:, 1, :]
    dev = pred - jnp.sum(pred, axis=0, keepdims=True) * (1.0 / pred.shape[0])
    scaled = dev / var_ref[...]
    sums_ref[...] = lax.dot_general(
        scaled,
        jnp.concatenate([dev, resid], axis=0),
        (((1,), (1,)), ((), ())),
        precision=lax.Precision.HIGHEST,
        preferred_element_type=jnp.float32,
    )


def whole_call(kernel, out_shape, *args):
    return pl.pallas_call(kernel, out_shape=out_shape, cost_estimate=LIGHT)(*args)


def solve_kernel(
    own_ref, far1_ref, far2_ref, far3_ref, x_ref, gain_ref, spread_ref, y_ref, x_buf, y_buf, x_sems, y_sems
):
    size = x_ref.shape[0] // LOADS
    loads = [
        pltpu.make_async_copy(
            x_ref.at[pl.ds(i * size, size)], x_buf.at[pl.ds(i * size, size)], x_sems.at[i]
        )
        for i in range(LOADS)
    ]
    for load in loads:
        load.start()
    total = (own_ref[...] + far1_ref[...]) + (far2_ref[...] + far3_ref[...])
    count = total.shape[0]
    row = lax.broadcasted_iota(jnp.int32, total.shape, 0)
    col = lax.broadcasted_iota(jnp.int32, total.shape, 1)
    total = total + jnp.where(row == col, float(count), 0.0)
    for k in range(count):
        pivot = total[k : k + 1, :] / total[k : k + 1, k : k + 1]
        total = jnp.where(row == k, pivot, total - total[:, k : k + 1] * pivot)
    gain = total[:, count:].astype(jnp.bfloat16)
    gain_ref[...] = gain
    size = count * ROWS
    row = lax.broadcasted_iota(jnp.int32, (size, count), 0)
    col = lax.broadcasted_iota(jnp.int32, (size, count), 1)
    expand = (row >> ROW_BITS == col).astype(jnp.bfloat16)
    wide = lax.dot_general(
        expand, gain, (((1,), (1,)), ((), ())), preferred_element_type=jnp.float32
    ).astype(jnp.bfloat16)
    wide = lax.dot_general(
        wide, expand, (((1,), (1,)), ((), ())), preferred_element_type=jnp.float32
    )
    at_row = lax.broadcasted_iota(jnp.int32, (size, size), 0)
    at_col = lax.broadcasted_iota(jnp.int32, (size, size), 1)
    same = ((at_row ^ at_col) & (ROWS - 1)) == 0
    spread_ref[...] = jnp.where(same, wide, 0.0).astype(jnp.bfloat16)

    for load in loads:
        load.wait()
    stores = []
    for i in range(x_ref.shape[1] // ROWS):
        rows = (slice(None), pl.ds(i * ROWS, ROWS), slice(None))
        apply_rows(spread_ref, x_buf, y_buf, i * ROWS)
        stores.append(pltpu.make_async_copy(y_buf.at[rows], y_ref.at[rows], y_sems.at[i]))
        stores[-1].start()
    for store in stores:
        store.wait()


def solve(sums, x):
    members = x.shape[0]
    size = members * ROWS
    vmem, anywhere = pl.BlockSpec(memory_space=pltpu.VMEM), pl.BlockSpec(memory_space=pl.ANY)
    return pl.pallas_call(
        solve_kernel,
        in_specs=[vmem] * len(sums) + [anywhere],
        out_specs=[vmem, vmem, anywhere],
        out_shape=[
            jax.ShapeDtypeStruct((members, members), jnp.bfloat16),
            jax.ShapeDtypeStruct((size, size), jnp.bfloat16),
            jax.ShapeDtypeStruct(x.shape, x.dtype),
        ],
        scratch_shapes=[
            pltpu.VMEM(x.shape, x.dtype),
            pltpu.VMEM(x.shape, x.dtype),
            pltpu.SemaphoreType.DMA((LOADS,)),
            pltpu.SemaphoreType.DMA((x.shape[1] // ROWS,)),
        ],
        compiler_params=pltpu.CompilerParams(vmem_limit_bytes=VMEM),
        cost_estimate=LIGHT,
    )(*sums, x)


def mix_plain(slab, gain_tr):
    full = slab.astype(jnp.float32)
    center = (full - jnp.mean(full, axis=0, keepdims=True)).astype(jnp.bfloat16)
    return jnp.einsum(
        "jk,krc->jrc", gain_tr, center, preferred_element_type=jnp.float32
    ).astype(jnp.bfloat16)


def mix_one(column, blocks):
    full = [block.astype(jnp.float32) for block in blocks]
    mean = sum(jnp.sum(block, axis=0) for block in full) * (1.0 / column.shape[0])
    total = jnp.zeros_like(mean)
    at = 0
    for block in full:
        count = block.shape[0]
        center = (block - mean).astype(jnp.bfloat16).astype(jnp.float32)
        total = total + jnp.sum(center * column[at : at + count, None, None], axis=0)
        at += count
    return total.astype(jnp.bfloat16)


def place_kernel(at_ref, *refs):
    parts, out_ref, sems = refs[:-2], refs[-2], refs[-1]
    size = parts[0].shape[0]
    copies = [
        pltpu.make_async_copy(
            part, out_ref.at[pl.ds((at_ref[0] ^ flip) * size, size)], sems.at[flip]
        )
        for flip, part in enumerate(parts)
    ]
    for copy in copies:
        copy.start()
    for copy in copies:
        copy.wait()


def place_parts(at, parts):
    count, shape = len(parts), parts[0].shape
    return pl.pallas_call(
        place_kernel,
        in_specs=[pl.BlockSpec(memory_space=pltpu.SMEM)]
        + [pl.BlockSpec(memory_space=pltpu.VMEM)] * count,
        out_specs=pl.BlockSpec(memory_space=pl.ANY),
        out_shape=jax.ShapeDtypeStruct((count * shape[0],) + shape[1:], parts[0].dtype),
        scratch_shapes=[pltpu.SemaphoreType.DMA((count,))],
        compiler_params=pltpu.CompilerParams(vmem_limit_bytes=32 << 20),
        cost_estimate=LIGHT,
    )(at[None], *parts)


def first_kernel(scale, x_ref, w_ref, b_ref, y_ref):
    summed = jnp.dot(x_ref[...], w_ref[...], preferred_element_type=jnp.float32)
    y = jax.nn.gelu(summed * scale + b_ref[...].astype(jnp.float32), approximate=True)
    y_ref[...] = y.astype(jnp.bfloat16)


def first_layer(x, w, b, part):
    rows, depth = x.shape
    half = w.shape[1] // 2
    step = min(TILE, half)
    first = part * (half // step)
    return pl.pallas_call(
        functools.partial(first_kernel, depth ** (-0.5)),
        grid=(half // step,),
        in_specs=[
            pl.BlockSpec((rows, depth), lambda i: (0, 0)),
            pl.BlockSpec((depth, step), lambda i: (0, i + first)),
            pl.BlockSpec((1, step), lambda i: (0, i + first)),
        ],
        out_specs=pl.BlockSpec((rows, step), lambda i: (0, i)),
        out_shape=jax.ShapeDtypeStruct((rows, half), jnp.bfloat16),
        compiler_params=pltpu.CompilerParams(vmem_limit_bytes=32 << 20),
        cost_estimate=LIGHT,
    )(x, w, b)


def second_kernel(scale, side_ref, *refs):
    inputs, weights, (b_ref, third_ref, y_ref) = refs[:4], refs[4:8], refs[8:]
    summed = sum(
        jnp.dot(x_ref[...], w_ref[...], preferred_element_type=jnp.float32)
        for x_ref, w_ref in zip(inputs, weights)
    )
    y = jax.nn.gelu(summed * scale + b_ref[...].astype(jnp.float32), approximate=True)
    part = lax.dot_general(
        third_ref[...],
        y.astype(jnp.bfloat16),
        (((1,), (1,)), ((), ())),
        preferred_element_type=jnp.float32,
    )

    @pl.when(pl.program_id(0) == 0)
    def _():
        y_ref[...] = jnp.zeros_like(y_ref)

    y_ref[...] += part * scale


def second_and_third(side, mine, other, w, b, third):
    rows, depth = mine[0].shape
    outs = third.shape[0]
    step = min(TILE, w.shape[1])
    whole = pl.BlockSpec((rows, depth), lambda i, side: (0, 0))
    return pl.pallas_call(
        functools.partial(second_kernel, w.shape[0] ** (-0.5)),
        grid_spec=pltpu.PrefetchScalarGridSpec(
            num_scalar_prefetch=1,
            grid=(w.shape[1] // step,),
            in_specs=[whole] * 4
            + [
                pl.BlockSpec((depth, step), lambda i, side: (2 * side[0], i)),
                pl.BlockSpec((depth, step), lambda i, side: (2 * side[0] + 1, i)),
                pl.BlockSpec((depth, step), lambda i, side: (2 - 2 * side[0], i)),
                pl.BlockSpec((depth, step), lambda i, side: (3 - 2 * side[0], i)),
                pl.BlockSpec((1, step), lambda i, side: (0, i)),
                pl.BlockSpec((outs, step), lambda i, side: (0, i)),
            ],
            out_specs=pl.BlockSpec((outs, rows), lambda i, side: (0, 0)),
        ),
        out_shape=jax.ShapeDtypeStruct((outs, rows), jnp.float32),
        compiler_params=pltpu.CompilerParams(vmem_limit_bytes=32 << 20),
        cost_estimate=LIGHT,
    )(side[None], *mine, *other, w, w, w, w, b, third)


def exchange(x):
    return lax.all_to_all(x, "member", split_axis=0, concat_axis=0, tiled=True)


def swap(x, axis, bit):
    count = lax.axis_size(axis)
    return lax.ppermute(x, axis, [(i, i ^ bit) for i in range(count)])


def reorder(gain_tr, order):
    pick = (order[None, :] == jnp.arange(gain_tr.shape[1])[:, None]).astype(jnp.bfloat16)
    return jnp.dot(gain_tr, pick, preferred_element_type=jnp.float32).astype(jnp.bfloat16)


def pick(x, at, axis=0):
    return lax.dynamic_index_in_dim(x, at, axis, keepdims=False)


def after(value, earlier):
    return lax.optimization_barrier((value, earlier))[0]


def body(samples, w_first, b_first, w_second, b_second, w_third, observed, perturb, variance):
    members = lax.axis_size("member")
    me = lax.axis_index("member")
    side = lax.axis_index("pair")
    width = w_first.shape[2]
    first_w, second_w, third_w = w_first[0], w_second[0], w_third[0]
    slabs_first = first_w.reshape(members, -1, width)
    slabs_second = second_w.reshape(members, -1, width)
    outs = third_w.shape[1]
    fast = members == PLANE * PLANE and width % TILE == 0
    planes = members // PLANE
    plane, place = me // PLANE, me % PLANE

    def across(x, flip):
        return swap(x, "member", flip * PLANE)

    first = [first_layer(samples, first_w, b_first, i) for i in range(2)]
    other = [swap(x, "pair", 1) for x in first]
    partial_out = second_and_third(side, first, other, second_w, b_second, third_w.T)

    half = partial_out.shape[1] // 2
    start = side * half
    keep = lax.dynamic_slice_in_dim(partial_out, start, half, 1)
    give = lax.dynamic_slice_in_dim(partial_out, (1 - side) * half, half, 1)
    pred = keep + swap(give, "pair", 1)
    observed_half = lax.dynamic_slice_in_dim(observed.T, start, half, 1)
    variance_half = lax.dynamic_slice_in_dim(variance.T, start, half, 1)
    perturb_half = lax.dynamic_slice_in_dim(perturb[0].T, start, half, 1)
    resid = observed_half + jnp.sqrt(variance_half) * perturb_half - pred
    count = pred.size // members
    both = jnp.concatenate(
        [pred.reshape(members, 1, count), resid.reshape(members, 1, count)], axis=1
    )
    got_second = exchange(slabs_second)
    var_part = lax.dynamic_index_in_dim(variance_half.reshape(members, count), me, 0)
    if fast:
        def by_plane(parts):
            parts = jnp.stack(parts)
            return jnp.stack([pick(parts, plane ^ i) for i in range(planes)])

        def within(x):
            parts = [pick(x, place ^ i, 1) for i in range(PLANE)]
            parts = jnp.stack([parts[0]] + [swap(parts[i], "member", i) for i in range(1, PLANE)])
            return jnp.stack([pick(parts, place ^ i) for i in range(PLANE)])

        slabs = after(slabs_first, partial_out)
        slabs = within(slabs.reshape((planes, PLANE) + slabs.shape[1:]))
        both = within(both.reshape((planes, PLANE) + both.shape[1:]))
        parts = [pick(both, plane ^ i, 1) for i in range(planes)]
        parts = [parts[0]] + [across(parts[i], i) for i in range(1, planes)]
        small = jnp.concatenate([third_w.T, b_first, b_second], axis=0)
        slabs = [pick(slabs, plane ^ i, 1) for i in range(planes)]
        joined = jnp.concatenate([slabs[2].reshape(-1, width), small], axis=0)
        center = blocked(center_kernel, got_second)
        parts, slabs, joined, center = lax.optimization_barrier((parts, slabs, joined, center))
        both = jnp.concatenate(by_plane(parts), axis=0)
        joined = across(joined, 2)
        size = joined.shape[0] - small.shape[0]
        held = [small[None], joined[None, size:]]
        parts = [
            slabs[0],
            across(slabs[1], 1),
            joined[:size].reshape(slabs[2].shape),
            across(slabs[3], 3),
        ]
        sums = whole_call(
            moments_kernel,
            jax.ShapeDtypeStruct((members, 2 * members), jnp.float32),
            both,
            var_part,
        )
        sums = sums + swap(sums, "pair", 1)
        sums = sums + swap(sums, "member", 1)
        sums = sums + swap(sums, "member", 2)
        sums, parts[1], parts[3] = lax.optimization_barrier((sums, parts[1], parts[3]))
        far = [across(sums, i) for i in range(1, planes)]
        far, held[1], parts = lax.optimization_barrier((far, held[1], parts))
        held.append(swap(jnp.concatenate(held, axis=0), "member", 4))
        gain, spread, mixed_second = solve([sums] + far, center)
        mixed_second, parts, held[2] = lax.optimization_barrier((mixed_second, parts, held[2]))
        new_second = exchange(mixed_second)

        held.append(swap(jnp.concatenate(held, axis=0), "member", 2))
        got_first = by_plane(parts).reshape(slabs_first.shape)
        mixed_first = blocked(mix_kernel, got_first, spread)
        mixed_first = mixed_first.reshape((planes, PLANE) + mixed_first.shape[1:])
        back, held[3] = lax.optimization_barrier((within(mixed_first), held[3]))
        held.append(swap(jnp.concatenate(held, axis=0), "member", 1))
        homes = [pick(back, plane ^ i, 1) for i in range(planes)]
        homes = [homes[0]] + [across(homes[i], i) for i in range(1, planes)]

        order = me[None]
        for bit in (8, 4, 2, 1):
            order = jnp.concatenate([order, order ^ bit])
        column = reorder(pick(gain, me, 1)[None], order)[0].astype(jnp.float32)
        new_small = mix_one(column, held)
        new_third = new_small[:outs].T
        new_bfirst = new_small[outs : outs + 1]
        new_bsecond = new_small[outs + 1 : outs + 2]
        new_second = blocked(copy_kernel, new_second)
        homes, new_second, new_third, new_bfirst, new_bsecond = lax.optimization_barrier(
            (homes, new_second, new_third, new_bfirst, new_bsecond)
        )
        new_first = place_parts(plane, homes)
    else:
        both = exchange(both)
        allpred, allres = both[:, 0], both[:, 1]
        devpred = allpred - jnp.mean(allpred, axis=0, keepdims=True)
        scaled = devpred / var_part
        sums = jnp.dot(
            scaled, jnp.concatenate([devpred, allres], axis=0).T, precision=lax.Precision.HIGHEST
        )
        sums = lax.psum(sums, ("member", "pair"))
        gain = solve_gain(sums[:, :members], sums[:, members:])
        gain_tr = gain.astype(jnp.bfloat16).T
        new_second = exchange(mix_plain(got_second, gain_tr))
        new_first = exchange(mix_plain(exchange(slabs_first), gain_tr))
        small = jnp.concatenate([third_w.T, b_first, b_second], axis=0)
        full = lax.all_gather(small, "member", axis=0)
        new_small = mix_plain(full, lax.dynamic_index_in_dim(gain_tr, me, 0))[0]
        new_third = new_small[:outs].T
        new_bfirst = new_small[outs : outs + 1]
        new_bsecond = new_small[outs + 1 :]
    return (
        new_first.reshape(w_first.shape),
        new_bfirst,
        new_second.reshape(w_second.shape),
        new_bsecond,
        new_third[None],
    )


def solution(mesh):
    in_specs = (
        P(),
        P("member", None, "pair"),
        P("member", "pair"),
        P("member", None, "pair"),
        P("member", "pair"),
        P("member", "pair", None),
        P(),
        P("member", None, None),
        P(),
    )
    out_specs = (
        P("member", None, "pair"),
        P("member", "pair"),
        P("member", None, "pair"),
        P("member", "pair"),
        P("member", "pair", None),
    )
    return jax.shard_map(body, mesh=mesh, in_specs=in_specs, out_specs=out_specs, check_vma=False)
```
